128 devices in a mesh: dp: 32 (over z, x_hi, y), mp: 4 (over x_lo, core).
Axes of the slice: x: 4 (x_hi: 2, x_lo: 2; x = x_hi * 2 + x_lo), y: 4, z: 4, core: 2. Of those that a mesh axis runs over, the one named last changes fastest.
Arguments:
- vit_partial: bfloat16 [4, 16384, 6144], P('mp', 'dp'), may hold values from -6 to 6
- vit_residual: bfloat16 [16384, 6144], P(('dp', 'mp')), may hold values from -6 to 6
- ln_gain: float32 [6144], replicated, may hold values from 0.5 to 1.5
- key_weight: bfloat16 [6144, 2048], P(None, 'mp'), may hold values from -0.078125 to 0.078125
- value_weight: bfloat16 [6144, 2048], P(None, 'mp'), may hold values from -0.078125 to 0.078125
- queries: bfloat16 [64, 512, 2048], P('dp', None, 'mp'), may hold values from -16 to 16
- context_grad: bfloat16 [64, 512, 2048], P('dp', None, 'mp'), may hold values from -6 to 6
- text_len: int32 [64], P('dp'), may hold values from 1 to 512
- image_pick: int32 [32, 2], P('dp'), may hold values from 0 to 1, each once within a row
Outputs:
- context: float32 [64, 512, 2048], P('dp', None, 'mp')
- query_grad: float32 [64, 512, 2048], P('dp', None, 'mp')
- key_weight_grad: float32 [6144, 2048], P('dp', 'mp')
- value_weight_grad: float32 [6144, 2048], P('dp', 'mp')
- stream_grad: float32 [16384, 6144], P(('dp', 'mp'))
The draws below stay inside these ranges and needn't reach their ends.
All inputs are finite; a program needn't handle non-finite values.
Results may differ from the reference program's by a relative error of at most 0.034.
Values may be sent and summed in bfloat16 or wider, within the bound.
No kernel may reach another device: no remote copies, remote signals or barrier semaphores. Data moves between devices by JAX's collectives and lax.ppermute only.
A program may use at most 192 MiB of HBM per device.

```python
import jax
import jax.numpy as jnp
from jax import lax

DV = 6144
HEADS = 8
HD = 256
VTOK = 256
TEXT = 512
IMG_DEV = 2
EXAMPLES = 64
ROWS = 16384
N_DP = 32
N_MP = 4


def draw_queries(key, part):
    key = jax.random.fold_in(key, 7)
    base_key = jax.random.fold_in(key, 0)
    values = jax.random.normal(base_key, (EXAMPLES, TEXT, HEADS * HD), jnp.float32)
    return jnp.clip(values, -16.0, 16.0).astype(jnp.bfloat16)


def with_ends(drawn, own_key, least, top_value):
    spot = [jax.random.randint(jax.random.fold_in(own_key, axis), (), 0, length) for axis, length in enumerate(drawn.shape)]
    main_axis = drawn.shape.index(max(drawn.shape))
    neighbour = spot[:main_axis] + [(spot[main_axis] + 1) % drawn.shape[main_axis]] + spot[main_axis + 1:]
    return drawn.at[tuple(spot)].set(least).at[tuple(neighbour)].set(top_value)


def raised(result, stream_key, source, target, blocks, factor):
    owner, partner = [(jnp.arange(result.shape[dim]) // (result.shape[dim] // blocks)).reshape([-1 if axis == dim else 1 for axis in range(result.ndim)]) for dim in (source, target)]
    chosen = jax.random.permutation(stream_key, blocks)[partner]
    strong = (owner == chosen) | (owner == (partner + blocks // 2) % blocks)
    return jnp.where(strong, factor * result, result)


def block_levels(own_key, shape, shards, least, largest):
    def one(axis_at, shards_of):
        heights = jax.random.uniform(jax.random.fold_in(jax.random.fold_in(own_key, 6), axis_at), (shards_of,), jnp.float32, least / len(shards), largest / len(shards))
        return jnp.repeat(jnp.exp(heights), shape[axis_at] // shards_of).reshape((-1,) + (1,) * (len(shape) - axis_at - 1))

    factor_of = one(*shards[0])
    for cut in shards[1:]:
        factor_of = factor_of * one(*cut)
    return factor_of


def noise(key, extent, scale, bound, pieces=(), kind=jnp.bfloat16):
    loudness = block_levels(key, extent, pieces, -0.22, 0.18) if pieces else 1.0
    drawn = jax.random.normal(key, extent, jnp.float32) * scale * loudness
    return jnp.minimum(jnp.maximum(drawn, -bound), bound).astype(kind)


def bell_draw_with(own_key, dims, scale, reach, cuts, heavy, kind=jnp.bfloat16):
    entries = scale * jax.random.normal(own_key, dims, jnp.float32)
    if cuts:
        entries = entries * block_levels(own_key, dims, cuts, -0.22, 0.18)
    return jnp.clip(raised(entries, jax.random.fold_in(own_key, 3), *heavy), -reach, reach).astype(kind)


def setup_inputs(seed: int = 0) -> dict:
    key_of = jax.random.split(jax.random.key(seed), 10)
    return {
        "vit_partial": bell_draw_with(key_of[0], (N_MP, ROWS, DV), 1.0, 6.0, ((0, 4), (1, 32)), (1, 2, 32, 2.75)),
        "vit_residual": noise(key_of[1], (ROWS, DV), 1.0, 6.0, ((0, 128),)),
        "ln_gain": jnp.clip(1.0 + 0.1 * jax.random.normal(key_of[2], (DV,), jnp.float32), 0.5, 1.5),
        "key_weight": noise(key_of[3], (DV, HEADS * HD), DV ** -0.5, 0.078125, ((1, 4),)),
        "value_weight": noise(key_of[4], (DV, HEADS * HD), DV ** -0.5, 0.078125, ((1, 4),)),
        "queries": draw_queries(jax.random.fold_in(key_of[9], 71), 0),
        "context_grad": noise(key_of[6], (EXAMPLES, TEXT, HEADS * HD), 1.0, 6.0, ((0, 32), (2, 4))),
        "text_len": with_ends(jax.random.randint(key_of[7], (EXAMPLES,), 1, TEXT + 1), jax.random.fold_in(key_of[7], 1), 1, TEXT).astype(jnp.int32),
        "image_pick": jax.vmap(lambda own: jax.random.permutation(own, IMG_DEV))(jax.random.split(key_of[8], N_DP)).reshape((N_DP, IMG_DEV)).astype(jnp.int32),
    }


def product(form, left, right):
    return jnp.einsum(form, left.astype(jnp.float32), right.astype(jnp.float32))

def layer_norm(stream, ln_gain):
    row_mean = lax.optimization_barrier(jnp.mean(stream, axis=-1, keepdims=True))
    centred = stream - row_mean
    inv_std = lax.rsqrt(lax.optimization_barrier(jnp.mean(centred * centred, axis=-1, keepdims=True)) + 1e-06)
    normal_rows = centred * inv_std
    return ((normal_rows * ln_gain).astype(jnp.bfloat16), normal_rows, inv_std)

def norm_backward(upstream, normal_rows, inv_std, ln_gain):
    scaled = upstream * ln_gain
    mean_grad = lax.optimization_barrier(jnp.mean(scaled, axis=-1, keepdims=True))
    mean_proj = lax.optimization_barrier(jnp.mean(scaled * normal_rows, axis=-1, keepdims=True))
    return inv_std * (scaled - mean_grad - normal_rows * mean_proj)

def cross_attention(visual_ex, key_weight, value_weight, queries, context_grad, text_len):
    examples, vis_tokens, model_width = visual_ex.shape
    text_rows, head_width = (queries.shape[1], queries.shape[2])
    head_count = head_width // HD
    flat_visual = visual_ex.reshape(examples * vis_tokens, model_width)
    key_rows = jnp.dot(flat_visual, key_weight, preferred_element_type=jnp.float32).astype(jnp.bfloat16)
    value_rows = jnp.dot(flat_visual, value_weight, preferred_element_type=jnp.float32).astype(jnp.bfloat16)
    key_rows = key_rows.reshape(examples, vis_tokens, head_count, HD)
    value_rows = value_rows.reshape(examples, vis_tokens, head_count, HD)
    query_rows = queries.reshape(examples, text_rows, head_count, HD)
    scores = product('eqhd,ekhd->ehqk', query_rows, key_rows) * HD ** (-0.5)
    row_top = lax.optimization_barrier(jnp.max(scores, axis=-1, keepdims=True))
    exp_terms = jnp.exp(scores - row_top)
    softmax_w = exp_terms / lax.optimization_barrier(jnp.sum(exp_terms, axis=-1, keepdims=True))
    weights_bf = softmax_w.astype(jnp.bfloat16)
    attended = product('ehqk,ekhd->eqhd', weights_bf, value_rows)
    text_mask = jnp.arange(text_rows, dtype=jnp.int32)[None, :] < text_len[:, None]
    context = attended * text_mask.astype(jnp.float32)[:, :, None, None]
    upstream = context_grad.reshape(examples, text_rows, head_count, HD) * text_mask.astype(jnp.bfloat16)[:, :, None, None]
    weight_grad = product('eqhd,ekhd->ehqk', upstream, value_rows)
    value_grad = product('ehqk,eqhd->ekhd', weights_bf, upstream).astype(jnp.bfloat16)
    centre = lax.optimization_barrier(jnp.sum(weight_grad * softmax_w, axis=-1, keepdims=True))
    score_grad = (softmax_w * (weight_grad - centre) * HD ** (-0.5)).astype(jnp.bfloat16)
    query_grad = product('ehqk,ekhd->eqhd', score_grad, key_rows)
    key_grad = product('ehqk,eqhd->ekhd', score_grad, query_rows).astype(jnp.bfloat16)
    return (context.reshape(examples, text_rows, head_width), query_grad.reshape(examples, text_rows, head_width), key_grad.reshape(examples * vis_tokens, head_width), value_grad.reshape(examples * vis_tokens, head_width))

def reference(vit_partial, vit_residual, ln_gain, key_weight, value_weight, queries, context_grad, text_len, image_pick):
    group_rows = IMG_DEV * VTOK
    head_cols = HEADS * HD // N_MP

    def one_group(weight_acc, group_idx):
        first_row = group_idx * group_rows
        partial_value = lax.dynamic_slice_in_dim(vit_partial, first_row, group_rows, 1).astype(jnp.float32)
        residual = lax.dynamic_slice_in_dim(vit_residual, first_row, group_rows, 0).astype(jnp.float32)
        stream = residual + lax.optimization_barrier(jnp.sum(partial_value, axis=0))
        visual, normal_rows, inv_std = layer_norm(stream, ln_gain)
        first_ex = group_idx * IMG_DEV
        image_order = lax.dynamic_slice_in_dim(image_pick, group_idx, 1, 0)[0]
        chooser = (image_order[:, None] == jnp.arange(IMG_DEV, dtype=jnp.int32)[None, :]).astype(jnp.float32)
        visual_ex = jnp.einsum('ei,itd->etd', chooser, visual.reshape(IMG_DEV, VTOK, DV).astype(jnp.float32)).astype(jnp.bfloat16)
        query_block = lax.dynamic_slice_in_dim(queries, first_ex, IMG_DEV, 0)
        grad_block = lax.dynamic_slice_in_dim(context_grad, first_ex, IMG_DEV, 0)
        length_rows = lax.dynamic_slice_in_dim(text_len, first_ex, IMG_DEV, 0)
        context, query_grad, key_grad, value_grad = cross_attention(visual_ex, key_weight, value_weight, query_block, grad_block, length_rows)
        flat_visual = visual_ex.reshape(group_rows, DV)
        both_grads = jnp.concatenate([key_grad, value_grad], axis=1)
        weight_acc = weight_acc + jnp.dot(flat_visual.T, both_grads, preferred_element_type=jnp.float32)
        visual_grad = jnp.zeros((group_rows, DV), jnp.float32)
        for member in range(N_MP):
            low = member * head_cols
            head_term = jnp.dot(key_grad[:, low:low + head_cols], key_weight[:, low:low + head_cols].T, preferred_element_type=jnp.float32)
            head_term = head_term + jnp.dot(value_grad[:, low:low + head_cols], value_weight[:, low:low + head_cols].T, preferred_element_type=jnp.float32)
            rounded = lax.optimization_barrier(head_term.astype(jnp.bfloat16))
            visual_grad = visual_grad + rounded.astype(jnp.float32)
        image_grad = jnp.einsum('ei,etd->itd', chooser, visual_grad.reshape(IMG_DEV, VTOK, DV))
        stream_grad = norm_backward(image_grad.reshape(group_rows, DV), normal_rows, inv_std, ln_gain)
        return (weight_acc, (context, query_grad, stream_grad))
    start_acc = jnp.zeros((DV, 2 * HEADS * HD), jnp.float32)
    weight_sum, stacked = lax.scan(one_group, start_acc, jnp.arange(N_DP, dtype=jnp.int32))
    context = stacked[0].reshape(EXAMPLES, TEXT, HEADS * HD)
    query_grad = stacked[1].reshape(EXAMPLES, TEXT, HEADS * HD)
    stream_grad = stacked[2].reshape(ROWS, DV)
    return (context, query_grad, weight_sum[:, :HEADS * HD], weight_sum[:, HEADS * HD:], stream_grad)
```

```python
import functools

import jax
import jax.numpy as jnp
from jax import lax
from jax.experimental import pallas as pl
from jax.experimental.pallas import tpu as pltpu
from jax.sharding import Mesh, PartitionSpec as P

HD = 256
BF = jnp.bfloat16
F32 = jnp.float32
SWAP = [(0, 1), (1, 0)]
NEAR = [(0, 1), (1, 0), (2, 3), (3, 2)]
WRAP = [(0, 3), (3, 0), (1, 2), (2, 1)]


def dot(left, right, dims=((1,), (0,))):
    return lax.dot_general(left, right, (dims, ((), ())), preferred_element_type=F32)


def pick_slice(array, index, dim):
    return lax.dynamic_index_in_dim(array, index, dim, keepdims=False)


def attention_body(first, pick_ref, len_ref, q_ref, g_ref, kv_ref, *rest):
    context_ref, query_grad_ref, grads_ref = rest[-3:]
    head = pl.program_id(0)
    heads = pl.num_programs(0)
    limit = len_ref[pick_ref[first]]
    q = q_ref[0]
    key = kv_ref[:, pl.ds(pl.multiple_of(head * HD, HD), HD)]
    value = kv_ref[:, pl.ds(pl.multiple_of((heads + head) * HD, HD), HD)]
    text_rows = q.shape[0]
    mask = lax.broadcasted_iota(jnp.int32, (text_rows, 1), 0) < limit
    scores = dot(q, key, ((1,), (1,))) * HD ** (-0.5)
    exp_terms = jnp.exp(scores - jnp.max(scores, axis=-1, keepdims=True))
    softmax_w = exp_terms / jnp.sum(exp_terms, axis=-1, keepdims=True)
    weights_bf = softmax_w.astype(BF)
    context_ref[0] = jnp.where(mask, dot(weights_bf, value), 0.0)
    upstream = jnp.where(mask, g_ref[0].astype(F32), 0.0).astype(BF)
    weight_grad = dot(upstream, value, ((1,), (1,)))
    centre = jnp.sum(weight_grad * softmax_w, axis=-1, keepdims=True)
    score_grad = (softmax_w * (weight_grad - centre) * HD ** (-0.5)).astype(BF)
    query_grad_ref[0] = dot(score_grad, key)
    key_grad = dot(score_grad, q, ((0,), (0,))).astype(BF)
    value_grad = dot(weights_bf, upstream, ((0,), (0,))).astype(BF)
    grads_ref[:, pl.ds(pl.multiple_of(head * HD, HD), HD)] = key_grad
    grads_ref[:, pl.ds(pl.multiple_of((heads + head) * HD, HD), HD)] = value_grad


def attention(image, pick, text_len, queries, context_grad, kv, partly):
    examples, text_rows, width = queries.shape
    heads = width // HD

    def by_example(head, pick_ref, len_ref):
        return (pick_ref[image], 0, head)

    def whole(head, pick_ref, len_ref):
        return (0, 0)

    text_block = pl.BlockSpec((1, text_rows, HD), by_example)
    flat_block = pl.BlockSpec(kv.shape, whole)
    out_text = jax.ShapeDtypeStruct(queries.shape, F32)
    aliases = {} if not partly else {5: 0, 6: 1}
    return pl.pallas_call(
        functools.partial(attention_body, image),
        grid_spec=pltpu.PrefetchScalarGridSpec(
            num_scalar_prefetch=2,
            grid=(heads,),
            in_specs=[text_block, text_block, flat_block]
            + [pl.BlockSpec(memory_space=pl.ANY)] * len(partly),
            out_specs=[text_block, text_block, flat_block],
        ),
        out_shape=[out_text, out_text, jax.ShapeDtypeStruct(kv.shape, BF)],
        input_output_aliases=aliases,
        compiler_params=pltpu.CompilerParams(vmem_limit_bytes=32 * 1024 * 1024),
        cost_estimate=pl.CostEstimate(
            flops=12 * text_rows * kv.shape[0] * width,
            bytes_accessed=12 * text_rows * width + 4 * kv.size,
            transcendentals=text_rows * kv.shape[0] * heads,
        ),
    )(pick, text_len, queries, context_grad, kv, *partly)


def ring_sum(parts, axis, dim, near_first):
    me = lax.axis_index(axis)
    near, wrap = me ^ 1, 3 - me
    if near_first:
        first, second, third = near, wrap, 3 - near
        swaps = (NEAR, WRAP)
    else:
        first, second, third = wrap, near, wrap ^ 1
        swaps = (WRAP, NEAR)
    sent = jnp.stack([pick_slice(parts, third, dim), pick_slice(parts, first, dim)])
    got = lax.ppermute(sent, axis, swaps[0])
    onward = (pick_slice(parts, second, dim).astype(F32) + got[0].astype(F32)).astype(BF)
    last = lax.ppermute(onward, axis, swaps[1])
    own = pick_slice(parts, me, dim).astype(F32) + got[1].astype(F32)
    return (own + last.astype(F32)).astype(BF)


def local(
    vit_partial,
    vit_residual,
    ln_gain,
    key_weight,
    value_weight,
    queries,
    context_grad,
    text_len,
    image_pick,
):
    share, model_width = vit_residual.shape
    width = key_weight.shape[1]
    core, side = lax.axis_index("c"), lax.axis_index("xl")
    partial = vit_partial[0].reshape(2, 2, share, model_width)
    weights = jnp.concatenate([key_weight, value_weight], axis=1)
    pick = image_pick[0]

    def chip_sum(image):
        theirs = lax.ppermute(pick_slice(partial[image], 1 - core, 0), "c", SWAP)
        total = pick_slice(partial[image], core, 0).astype(F32) + theirs.astype(F32)
        return (total + jnp.where(side == image, vit_residual.astype(F32), 0.0)).astype(BF)

    def normal(stream):
        row_mean = jnp.mean(stream, axis=-1, keepdims=True)
        centred = stream - row_mean
        inv_std = lax.rsqrt(jnp.mean(centred * centred, axis=-1, keepdims=True) + 1e-06)
        return centred * inv_std, inv_std

    mine = [chip_sum(image) for image in range(2)]
    other = [lax.ppermute(total, "xl", SWAP) for total in mine]
    texts, visual, grads = [], [], []
    for image in range(2):
        normal_rows, _ = normal(mine[image].astype(F32) + other[image].astype(F32))
        half = (normal_rows * ln_gain).astype(BF)
        visual.append(jnp.concatenate([half, lax.ppermute(half, "c", SWAP)], axis=0))
        kv = dot(visual[image], weights).astype(BF)
        context, query_grad, both = attention(
            image, pick, text_len, queries, context_grad, kv, texts
        )
        texts = [context, query_grad]
        grads.append(both)

    parts = []
    for block in range(2 * width // HD):
        columns = slice(block * HD, (block + 1) * HD)
        term = dot(visual[0], grads[0][:, columns], ((0,), (0,)))
        term = term + dot(visual[1], grads[1][:, columns], ((0,), (0,)))
        parts.append(term.astype(BF).reshape(4, 2, 4, model_width // 32, HD))
    sums = []
    for block, part in enumerate(parts):
        near = block < 2
        if block % 2 == 0:
            sums.append(ring_sum(ring_sum(part, "y", 2, near), "z", 0, near))
        else:
            sums.append(ring_sum(ring_sum(part, "z", 0, near), "y", 1, near))
    sums = jnp.stack(sums)
    half_index = lax.axis_index("xh")
    got = lax.ppermute(pick_slice(sums, 1 - half_index, 1), "xh", SWAP)
    weight_grads = pick_slice(sums, half_index, 1).astype(F32) + got.astype(F32)
    key_weight_grad = jnp.concatenate([weight_grads[0], weight_grads[1]], axis=1)
    value_weight_grad = jnp.concatenate([weight_grads[2], weight_grads[3]], axis=1)

    shares = []
    for image in range(2):
        visual_grad = dot(grads[image], weights, ((1,), (1,))).astype(BF)
        theirs = lax.ppermute(visual_grad[share:], "c", SWAP)
        shares.append(visual_grad[:share].astype(F32) + theirs.astype(F32))
    sent = jnp.where(side == 0, shares[1], shares[0]).astype(BF)
    got = lax.ppermute(sent, "xl", SWAP)
    image_grad = jnp.where(side == 0, shares[0], shares[1]) + got.astype(F32)
    stream = jnp.where(
        side == 0,
        mine[0].astype(F32) + other[0].astype(F32),
        mine[1].astype(F32) + other[1].astype(F32),
    )
    normal_rows, inv_std = normal(stream)
    scaled = image_grad * ln_gain
    mean_grad = jnp.mean(scaled, axis=-1, keepdims=True)
    mean_proj = jnp.mean(scaled * normal_rows, axis=-1, keepdims=True)
    stream_grad = inv_std * (scaled - mean_grad - normal_rows * mean_proj)
    return texts[0], texts[1], key_weight_grad, value_weight_grad, stream_grad


def solution(mesh):
    fine = Mesh(mesh.devices.reshape(4, 2, 4, 2, 2), ("z", "xh", "y", "xl", "c"))
    dp, mp = ("z", "xh", "y"), ("xl", "c")
    placed = (
        P(mp, dp, None),
        P(dp + mp, None),
        P(),
        P(None, mp),
        P(None, mp),
        P(dp, None, mp),
        P(dp, None, mp),
        P(dp),
        P(dp, None),
    )
    return jax.shard_map(
        local,
        mesh=fine,
        in_specs=placed,
        out_specs=(P(dp, None, mp), P(dp, None, mp), P(dp, mp), P(dp, mp), P(dp + mp, None)),
        check_vma=False,
    )
```

```python
import functools

import jax
import jax.numpy as jnp
from jax import lax
from jax.experimental import pallas as pl
from jax.experimental.pallas import tpu as pltpu
from jax.sharding import Mesh, PartitionSpec as P

HD = 256
RING = 4
BF = jnp.bfloat16
F32 = jnp.float32
SWAP = [(0, 1), (1, 0)]
MIB = 1024 * 1024
LANES = 512
CUTS = 4
ANYWHERE = pl.BlockSpec(memory_space=pl.ANY)


def dot(left, right, dims=((1,), (0,))):
    return lax.dot_general(left, right, (dims, ((), ())), preferred_element_type=F32)


def shape(dims, kind=BF):
    return jax.ShapeDtypeStruct(dims, kind)


def cost(flops, moved, special=0):
    return pl.CostEstimate(flops=flops, bytes_accessed=moved, transcendentals=special)


def call(body, grid, scalars, ins, in_specs, outs, out_specs, scratch=(), after=(), mib=20, **more):
    count, waits = len(scalars) + len(ins), len(after)

    def with_waits(*refs):
        body(*refs[:count], *refs[count + waits :])

    return pl.pallas_call(
        with_waits,
        grid_spec=pltpu.PrefetchScalarGridSpec(
            num_scalar_prefetch=len(scalars),
            grid=grid,
            in_specs=list(in_specs) + [ANYWHERE] * waits,
            out_specs=out_specs,
            scratch_shapes=scratch,
        ),
        out_shape=outs,
        compiler_params=pltpu.CompilerParams(vmem_limit_bytes=mib * MIB),
        **more,
    )(*scalars, *ins, *after)


def part_of_body(image, where_ref, part_in, share_in, out, hold, load_sems, store_sems):
    rows = out.shape[0]
    step = rows // 4
    start = (image * 2 + 1 - where_ref[0]) * rows

    def load(n):
        source = part_in.at[0, pl.ds(pl.multiple_of(start + n * step, step), step)]
        return pltpu.make_async_copy(source, hold.at[pl.ds(n * step, step)], load_sems.at[n])

    def store(n):
        at = pl.ds(n * step, step)
        return pltpu.make_async_copy(hold.at[at], out.at[at], store_sems.at[n])

    for n in range(4):
        load(n).start()
    for n in range(4):
        load(n).wait()
        store(n).start()
    for n in range(4):
        store(n).wait()


def part_of(image, where, vit_partial, vit_residual, after):
    return call(
        functools.partial(part_of_body, image),
        (1,),
        [where],
        [vit_partial, vit_residual],
        [ANYWHERE] * 2,
        shape(vit_residual.shape),
        ANYWHERE,
        scratch=[
            pltpu.VMEM(vit_residual.shape, BF),
            pltpu.SemaphoreType.DMA((4,)),
            pltpu.SemaphoreType.DMA((4,)),
        ],
        after=after,
        mib=60,
    )


def lanes(width):
    return [slice(start, start + LANES) for start in range(0, width, LANES)]


def chip_sum_body(image, where_ref, part_ref, theirs_ref, residual_ref, out_ref):
    scale = jnp.where(where_ref[1] == image, 1.0, 0.0)
    for at in lanes(out_ref.shape[1]):
        total = part_ref[0, :, at].astype(F32) + theirs_ref[:, at].astype(F32)
        out_ref[:, at] = (total + scale * residual_ref[:, at].astype(F32)).astype(BF)


def chip_sum(image, where, vit_partial, theirs, residual):
    rows, width = residual.shape
    step = rows // 4
    plain = pl.BlockSpec((step, width), lambda i, where_ref: (i, 0))
    return call(
        functools.partial(chip_sum_body, image),
        (4,),
        [where],
        [vit_partial, theirs, residual],
        [
            pl.BlockSpec(
                (1, step, width), lambda i, where_ref: (0, (image * 2 + where_ref[0]) * 4 + i, 0)
            ),
            plain,
            plain,
        ],
        shape((rows, width)),
        plain,
        cost_estimate=cost(0, 8 * rows * width),
    )


def centre_rows(first_ref, second_ref, hold_ref, rows):
    width = hold_ref.shape[1]
    total = 0.0
    for at in lanes(width):
        stream = first_ref[rows, at].astype(F32) + second_ref[rows, at].astype(F32)
        hold_ref[rows, at] = stream
        total = total + stream
    row_mean = jnp.sum(total, axis=-1, keepdims=True) * (1.0 / width)
    total = 0.0
    for at in lanes(width):
        centred = hold_ref[rows, at] - row_mean
        hold_ref[rows, at] = centred
        total = total + centred * centred
    return lax.rsqrt(jnp.sum(total, axis=-1, keepdims=True) * (1.0 / width) + 1e-06)


def norm_body(mine_ref, other_ref, gain_ref, out_ref, hold_ref):
    rows = slice(None)
    inv_std = centre_rows(mine_ref, other_ref, hold_ref, rows)
    for at in lanes(out_ref.shape[1]):
        out_ref[:, at] = (hold_ref[:, at] * inv_std * gain_ref[:, at]).astype(BF)


def norm(mine, other, gain, after):
    rows, width = mine.shape
    plain = pl.BlockSpec((rows // 4, width), lambda i: (i, 0))
    return call(
        norm_body,
        (4,),
        [],
        [mine, other, gain],
        [plain, plain, pl.BlockSpec((1, width), lambda i: (0, 0))],
        shape((rows, width)),
        plain,
        scratch=[pltpu.VMEM((rows // 4, width), F32)],
        after=after,
        cost_estimate=cost(0, 6 * rows * width),
    )


def norm_back_body(where_ref, gain_ref, *refs):
    first, second = refs[:4], refs[4:8]
    out, held, hold, result, load_sems, store_sems = refs[8:]
    width = hold.shape[1]
    rows = held.shape[1] // 4

    def loads(n, group):
        at = pl.ds(n * rows, rows)
        return [
            pltpu.make_async_copy(source.at[at], held.at[j, at], load_sems.at[j, n])
            for j, source in enumerate(group)
        ]

    for side, group in enumerate((first, second)):

        @pl.when(where_ref[1] == side)
        def _(group=group):
            for n in range(4):
                for copy in loads(n, group):
                    copy.start()

    stores = []
    for n in range(4):
        for copy in loads(n, first):
            copy.wait()
        part = slice(n * rows, (n + 1) * rows)
        inv_std = centre_rows(held.at[0], held.at[1], hold, part)
        sum_grad = sum_proj = 0.0
        for at in lanes(width):
            scaled = held[2, part, at].astype(F32) + held[3, part, at].astype(F32)
            scaled = scaled * gain_ref[:, at]
            result[part, at] = scaled
            sum_grad = sum_grad + scaled
            sum_proj = sum_proj + scaled * hold[part, at]
        mean_grad = jnp.sum(sum_grad, axis=-1, keepdims=True) * (1.0 / width)
        mean_proj = jnp.sum(sum_proj, axis=-1, keepdims=True) * inv_std * (1.0 / width)
        for at in lanes(width):
            normal_rows = hold[part, at] * inv_std
            result[part, at] = inv_std * (result[part, at] - mean_grad - normal_rows * mean_proj)
        at = pl.ds(n * rows, rows)
        stores.append(pltpu.make_async_copy(result.at[at], out.at[at], store_sems.at[n]))
        stores[n].start()
    for copy in stores:
        copy.wait()


def norm_back(where, gain, first, second):
    rows, width = first[0].shape
    return call(
        norm_back_body,
        (1,),
        [where],
        [gain, *first, *second],
        [pl.BlockSpec((1, width), lambda i, where_ref: (0, 0))] + [ANYWHERE] * 8,
        shape((rows, width), F32),
        ANYWHERE,
        scratch=[
            pltpu.VMEM((4, rows, width), BF),
            pltpu.VMEM((rows, width), F32),
            pltpu.VMEM((rows, width), F32),
            pltpu.SemaphoreType.DMA((4, 4)),
            pltpu.SemaphoreType.DMA((4,)),
        ],
        cost_estimate=cost(0, 12 * rows * width),
    )


def ring_sum_body(where_ref, *refs):
    kept_ref, sent_ref = refs[RING:]
    rows = kept_ref.shape[0]

    def total(block):
        at = pl.ds(pl.multiple_of(block * rows, rows), rows)
        return sum(ref[at].astype(F32) for ref in refs[:RING])

    sent_ref[...] = total(1 - where_ref[4]).astype(BF)
    kept_ref[...] = total(where_ref[4])


def ring_sum(where, blocks, after):
    rows, width = blocks[0].shape
    whole = pl.BlockSpec((rows, width), lambda i, where_ref: (0, 0))
    half = pl.BlockSpec((rows // 2, width), lambda i, where_ref: (0, 0))
    return call(
        ring_sum_body,
        (1,),
        [where],
        blocks,
        [whole] * RING,
        [shape((rows // 2, width), F32), shape((rows // 2, width))],
        [half, half],
        after=after,
        cost_estimate=cost(0, 12 * rows * width),
    )


def last_sum_body(kept_ref, got_ref, key_ref, value_ref):
    total = kept_ref[...] + got_ref[...].astype(F32)
    width = key_ref.shape[1]
    key_ref[...] = total[:, :width]
    value_ref[...] = total[:, width:]


def last_sum(kept, got):
    rows, width = kept.shape
    whole = pl.BlockSpec((rows, width), lambda i: (0, 0))
    half = pl.BlockSpec((rows, width // 2), lambda i: (0, 0))
    return call(
        last_sum_body,
        (1,),
        [],
        [kept, got],
        [whole, whole],
        [shape((rows, width // 2), F32)] * 2,
        [half, half],
        cost_estimate=cost(0, 10 * rows * width),
    )


def strips_body(where_ref, own_in, far_in, *rest):
    outs = rest[:RING]
    own_ref, far_ref, hold, load_sems, store_sems = rest[RING:]
    total_rows, width = own_ref.shape
    step = total_rows // 4
    piece = width // (2 * RING * RING)
    refs = (own_ref, far_ref)

    def load(n, half):
        at = pl.ds(n * step, step)
        source = (own_in, far_in)[half]
        return pltpu.make_async_copy(source.at[at], refs[half].at[at], load_sems.at[half, n])

    def store(n, k):
        at = pl.ds(n * step, step)
        source = hold.at[lax.rem(where_ref[2] + k, RING)]
        return pltpu.make_async_copy(source.at[:, at], outs[k].at[:, at], store_sems.at[k, n])

    def fill(n, along_y):
        at = slice(n * step, (n + 1) * step)
        for half in range(2):
            for a in range(RING):
                for b in range(RING):
                    for x in range(2):
                        z, y = (b, a) if along_y else (a, b)
                        start = ((z * 2 + x) * RING + y) * piece
                        spot = (b * 2 + x) * piece
                        hold[a, half, at, spot : spot + piece] = refs[half][at, start : start + piece]

    for n in range(4):
        for half in range(2):
            load(n, half).start()
    for n in range(4):
        for half in range(2):
            load(n, half).wait()
        pl.when(where_ref[0] == 0)(functools.partial(fill, n, True))
        pl.when(where_ref[0] == 1)(functools.partial(fill, n, False))
        for k in range(RING):
            store(n, k).start()
    for n in range(4):
        for k in range(RING):
            store(n, k).wait()


def strips(where, own, far, after):
    rows, width = own.shape
    part = width // RING
    return call(
        strips_body,
        (1,),
        [where],
        [own, far],
        [ANYWHERE] * 2,
        [shape((2, rows, part))] * RING,
        [ANYWHERE] * RING,
        scratch=[
            pltpu.VMEM((rows, width), BF),
            pltpu.VMEM((rows, width), BF),
            pltpu.VMEM((RING, 2, rows, part), BF),
            pltpu.SemaphoreType.DMA((2, 4)),
            pltpu.SemaphoreType.DMA((RING, 4)),
        ],
        after=after,
        cost_estimate=cost(0, 8 * rows * width),
    )


def image_body(image, pick_ref, len_ref, own_in, far_in, key_in, value_in, q_in, g_in, *rest):
    context_out, query_grad_out, near_out, away_out, grads_ref = rest[-19:-14]
    rows, keys, values, total, q_ref, g_ref, context_ref, query_grad_ref, back = rest[-14:-5]
    row_sems, weight_sems, text_sems, back_sems, done_sems = rest[-5:]
    half = rows.shape[0] // 2
    chunk = keys.shape[0] // CUTS
    width = keys.shape[1]
    example = pick_ref[image]
    limit = len_ref[example]

    def at(n):
        return pl.ds(pl.multiple_of(n * chunk, chunk), chunk)

    def row_loads(n):
        return [
            pltpu.make_async_copy(own_in.at[:, at(n)], rows.at[:half, at(n)], row_sems.at[0, n]),
            pltpu.make_async_copy(far_in.at[:, at(n)], rows.at[half:, at(n)], row_sems.at[1, n]),
        ]

    def weight_loads(n):
        return [
            pltpu.make_async_copy(key_in.at[at(n)], keys.at[at(n)], weight_sems.at[0, n]),
            pltpu.make_async_copy(value_in.at[at(n)], values.at[at(n)], weight_sems.at[1, n]),
        ]

    def back_stores(n):
        return [
            pltpu.make_async_copy(back.at[:half, at(n)], near_out.at[:, at(n)], back_sems.at[0, n]),
            pltpu.make_async_copy(back.at[half:, at(n)], away_out.at[:, at(n)], back_sems.at[1, n]),
        ]

    text_loads = [
        pltpu.make_async_copy(q_in.at[example], q_ref, text_sems.at[0]),
        pltpu.make_async_copy(g_in.at[example], g_ref, text_sems.at[1]),
    ]
    text_stores = [
        pltpu.make_async_copy(context_ref, context_out.at[example], done_sems.at[0]),
        pltpu.make_async_copy(query_grad_ref, query_grad_out.at[example], done_sems.at[1]),
    ]

    @pl.loop(0, CUTS)
    def _(n):
        for copy in row_loads(n) + weight_loads(n):
            copy.start()

    for copy in text_loads:
        copy.start()
    total[...] = jnp.zeros_like(total)

    @pl.loop(0, CUTS)
    def _(n):
        for copy in row_loads(n) + weight_loads(n):
            copy.wait()
        left = rows[:, at(n)]
        total[:, :width] += dot(left, keys[at(n)])
        total[:, width:] += dot(left, values[at(n)])

    for copy in text_loads:
        copy.wait()
    mask = lax.broadcasted_iota(jnp.int32, (q_ref.shape[0], 1), 0) < limit
    for head in range(width // HD):
        key_at = slice(head * HD, (head + 1) * HD)
        value_at = slice(width + head * HD, width + (head + 1) * HD)
        key, value = total[:, key_at].astype(BF), total[:, value_at].astype(BF)
        q = q_ref[:, key_at]
        scores = dot(q, key, ((1,), (1,))) * HD ** (-0.5)
        exp_terms = jnp.exp(scores - jnp.max(scores, axis=-1, keepdims=True))
        softmax_w = exp_terms / jnp.sum(exp_terms, axis=-1, keepdims=True)
        weights_bf = softmax_w.astype(BF)
        context_ref[:, key_at] = jnp.where(mask, dot(weights_bf, value), 0.0)
        upstream = jnp.where(mask, g_ref[:, key_at].astype(F32), 0.0).astype(BF)
        weight_grad = dot(upstream, value, ((1,), (1,)))
        centre = jnp.sum(weight_grad * softmax_w, axis=-1, keepdims=True)
        score_grad = (softmax_w * (weight_grad - centre) * HD ** (-0.5)).astype(BF)
        query_grad_ref[:, key_at] = dot(score_grad, key)
        grads_ref[:, key_at] = dot(score_grad, q, ((0,), (0,))).astype(BF)
        grads_ref[:, value_at] = dot(weights_bf, upstream, ((0,), (0,))).astype(BF)
    for copy in text_stores:
        copy.start()

    @pl.loop(0, CUTS)
    def _(n):
        term = dot(grads_ref[:, :width], keys[at(n)], ((1,), (1,)))
        term = term + dot(grads_ref[:, width:], values[at(n)], ((1,), (1,)))
        back[:, at(n)] = term.astype(BF)
        for copy in back_stores(n):
            copy.start()

    @pl.loop(0, CUTS)
    def _(n):
        for copy in back_stores(n):
            copy.wait()

    for copy in text_stores:
        copy.wait()


def image_step(
    image, pick, text_len, own, far, key_weight, value_weight, queries, context_grad, partly, after
):
    text_rows, width = queries.shape[1:]
    half, depth = own.shape
    flat = (2 * half, 2 * width)
    sems = pltpu.SemaphoreType.DMA
    return call(
        functools.partial(image_body, image),
        (1,),
        [pick, text_len],
        [own, far, key_weight, value_weight, queries, context_grad, *partly],
        [ANYWHERE] * (6 + len(partly)),
        [shape(queries.shape, F32)] * 2 + [shape(own.shape)] * 2 + [shape(flat)],
        [ANYWHERE] * 4 + [pl.BlockSpec(flat, lambda i, *scalars: (0, 0))],
        scratch=[
            pltpu.VMEM((2 * half, depth), BF),
            pltpu.VMEM(key_weight.shape, BF),
            pltpu.VMEM(key_weight.shape, BF),
            pltpu.VMEM(flat, F32),
            pltpu.VMEM((text_rows, width), BF),
            pltpu.VMEM((text_rows, width), BF),
            pltpu.VMEM((text_rows, width), F32),
            pltpu.VMEM((text_rows, width), F32),
            pltpu.VMEM((2 * half, depth), BF),
            sems((2, CUTS)),
            sems((2, CUTS)),
            sems((2,)),
            sems((2, CUTS)),
            sems((2,)),
        ],
        after=after,
        input_output_aliases={8: 0, 9: 1} if partly else {},
        mib=44,
        cost_estimate=cost(
            16 * half * depth * width + 24 * text_rows * half * width,
            4 * depth * (2 * half + width) + 12 * text_rows * width,
            2 * text_rows * half * width // HD,
        ),
    )


def weight_grad_body(first, where_ref, *refs):
    lefts_in, rights_in, rest = refs[:RING], refs[RING : 2 * RING], refs[2 * RING :]
    left, right, result, left_sems, right_sems, store_sems = rest[-6:]
    outs = rest[:1] if first else rest[1 : 1 + RING]
    rows = right.shape[0] // RING
    chunk, width = result.shape[1:]
    half = rows // 2
    wide = width // 2

    def right_load(k):
        at = pl.ds(k * rows, rows)
        return pltpu.make_async_copy(rights_in[k], right.at[at], right_sems.at[k])

    def left_load(n, k, h):
        columns = pl.ds(pl.multiple_of(lax.rem(where_ref[3] + n, RING) * chunk, chunk), chunk)
        at = pl.ds(k * rows + h * half, half)
        source = lefts_in[k].at[h, :, columns]
        return pltpu.make_async_copy(source, left.at[n, at], left_sems.at[n, k, h])

    def store(n):
        target = outs[0].at[n] if first else outs[n]
        return pltpu.make_async_copy(result.at[n], target, store_sems.at[n])

    each = [(k, h) for k in range(RING) for h in range(2)]
    for k in range(RING):
        right_load(k).start()
    for n in range(RING):
        for k, h in each:
            left_load(n, k, h).start()
    for k in range(RING):
        right_load(k).wait()
    for n in range(RING):
        for k, h in each:
            left_load(n, k, h).wait()
        for columns in (slice(0, wide), slice(wide, width)):
            total = dot(left[n], right[:, columns], ((0,), (0,)))
            if not first:
                total = total + rest[0][n, :, columns].astype(F32)
            result[n, :, columns] = total.astype(BF)
        store(n).start()
    for n in range(RING):
        store(n).wait()


def weight_grad(where, lefts, rights, so_far=None, after=()):
    halves, rows, part = lefts[0].shape
    width = rights[0].shape[1]
    chunk = part // RING
    first = so_far is None
    whole = (RING, chunk, width)
    return call(
        functools.partial(weight_grad_body, first),
        (1,),
        [where],
        [*lefts, *rights] + ([] if first else [so_far]),
        [ANYWHERE] * (2 * RING)
        + ([] if first else [pl.BlockSpec(whole, lambda i, where_ref: (0, 0, 0))]),
        [shape(whole)] if first else [shape(whole[1:])] * RING,
        [ANYWHERE] if first else [ANYWHERE] * RING,
        scratch=[
            pltpu.VMEM((RING, RING * halves * rows, chunk), BF),
            pltpu.VMEM((RING * halves * rows, width), BF),
            pltpu.VMEM(whole, BF),
            pltpu.SemaphoreType.DMA((RING, RING, 2)),
            pltpu.SemaphoreType.DMA((RING,)),
            pltpu.SemaphoreType.DMA((RING,)),
        ],
        after=after,
        cost_estimate=cost(
            4 * RING * halves * rows * part * width, 2 * RING * (part + width) * 2 * rows
        ),
    )


def later(array, after):
    return call(
        lambda *refs: None,
        (1,),
        [],
        [array],
        [ANYWHERE],
        shape(array.shape, array.dtype),
        ANYWHERE,
        after=after,
        input_output_aliases={0: 0},
    )


def hop(first, distance):
    pairs = []
    for z in range(RING):
        for y in range(RING):
            for core in range(2):
                along_y = (core == 0) == first
                to = (z, (y + distance) % RING) if along_y else ((z + distance) % RING, y)
                pairs.append(((z * RING + y) * 2 + core, (to[0] * RING + to[1]) * 2 + core))
    return pairs


def rotate(array, first, distance):
    return lax.ppermute(array, ("z", "y", "c"), hop(first, distance))


def local(
    vit_partial,
    vit_residual,
    ln_gain,
    key_weight,
    value_weight,
    queries,
    context_grad,
    text_len,
    image_pick,
):
    share, model_width = vit_residual.shape
    width = key_weight.shape[1]
    core, side, cross = lax.axis_index("c"), lax.axis_index("xl"), lax.axis_index("xh")
    y, z = lax.axis_index("y"), lax.axis_index("z")
    where = jnp.stack([core, side, jnp.where(core == 0, y, z), jnp.where(core == 0, z, y), cross])
    pick = image_pick[0]
    gain = ln_gain[None, :]

    mine, other, after = [], [], []
    for image in range(2):
        sent = part_of(image, where, vit_partial, vit_residual, after)
        after = [sent]
        theirs = lax.ppermute(sent, "c", SWAP)
        mine.append(chip_sum(image, where, vit_partial, theirs, vit_residual))
        other.append(lax.ppermute(mine[image], "xl", SWAP))

    def spread(array, firsts):
        return [array] + [rotate(firsts[k], True, k) for k in range(1, RING)]

    def core_sum(near_rows, away_rows):
        theirs = lax.ppermute(away_rows, "c", SWAP)
        return (near_rows.astype(F32) + theirs.astype(F32)).astype(BF)

    def step(image, own, far, texts, after):
        given = (key_weight, value_weight, queries, context_grad)
        return image_step(image, pick, text_len, own, far, *given, texts, after)

    own = norm(mine[0], other[0], gain, [mine[1]])
    far = lax.ppermute(own, "c", SWAP)
    pieces = strips(where, own, far, [])
    lefts = spread(pieces[0], pieces)
    *texts, near_rows, away_rows, grads = step(0, own, far, [], [pieces[0]])
    grads = later(grads, lefts[1:])
    rights = spread(grads, [grads] * RING)

    own = norm(mine[1], other[1], gain, [near_rows, rights[1], rights[3]])
    far = lax.ppermute(own, "c", SWAP)
    pieces = strips(where, own, far, [rights[2]])
    share_0 = core_sum(near_rows, later(away_rows, [pieces[0]]))
    last_lefts = spread(pieces[0], pieces)
    *texts, near_rows, away_rows, grads = step(1, own, far, texts, [pieces[0]])
    grads = later(grads, last_lefts[1:])
    last_rights = spread(grads, [grads] * RING)
    share_1 = core_sum(near_rows, later(away_rows, [grads]))
    (so_far,) = weight_grad(where, lefts, rights, after=[near_rows])

    from_second = lax.ppermute(share_0, "xl", [(1, 0)])
    from_first = lax.ppermute(share_1, "xl", [(0, 1)])
    blocks = weight_grad(where, last_lefts, last_rights, so_far, [share_0, share_1])
    got = [rotate(blocks[k], False, k) for k in range(1, RING)]
    stream_grad = norm_back(
        where,
        gain,
        [mine[0], other[0], share_0, from_second],
        [mine[1], other[1], share_1, from_first],
    )
    kept, sent = ring_sum(where, [blocks[0], *got], [stream_grad])
    got = lax.ppermute(sent, "xh", SWAP)
    key_weight_grad, value_weight_grad = last_sum(kept, got)
    return texts[0], texts[1], key_weight_grad, value_weight_grad, stream_grad


def solution(mesh):
    fine = Mesh(mesh.devices.reshape(4, 2, 4, 2, 2), ("z", "xh", "y", "xl", "c"))
    dp, mp = ("z", "xh", "y"), ("xl", "c")
    placed = (
        P(mp, dp, None),
        P(dp + mp, None),
        P(),
        P(None, mp),
        P(None, mp),
        P(dp, None, mp),
        P(dp, None, mp),
        P(dp),
        P(dp, None),
    )
    return jax.shard_map(
        local,
        mesh=fine,
        in_specs=placed,
        out_specs=(P(dp, None, mp), P(dp, None, mp), P(dp, mp), P(dp, mp), P(dp + mp, None)),
        check_vma=False,
    )
```

```python
import functools

import jax
import jax.numpy as jnp
from jax import lax
from jax.experimental import pallas as pl
from jax.experimental.pallas import tpu as pltpu
from jax.sharding import Mesh, PartitionSpec as P

HD = 256
RING = 4
BF = jnp.bfloat16
F32 = jnp.float32
SWAP = [(0, 1), (1, 0)]
MIB = 1024 * 1024
LANES = 512
CUTS = 4
ANYWHERE = pl.BlockSpec(memory_space=pl.ANY)


def dot(left, right, dims=((1,), (0,))):
    return lax.dot_general(left, right, (dims, ((), ())), preferred_element_type=F32)


def shape(dims, kind=BF):
    return jax.ShapeDtypeStruct(dims, kind)


def cost(flops, moved, special=0):
    return pl.CostEstimate(flops=flops, bytes_accessed=moved, transcendentals=special)


def call(body, grid, scalars, ins, in_specs, outs, out_specs, scratch=(), after=(), mib=20, **more):
    count, waits = len(scalars) + len(ins), len(after)

    def with_waits(*refs):
        body(*refs[:count], *refs[count + waits :])

    return pl.pallas_call(
        with_waits,
        grid_spec=pltpu.PrefetchScalarGridSpec(
            num_scalar_prefetch=len(scalars),
            grid=grid,
            in_specs=list(in_specs) + [ANYWHERE] * waits,
            out_specs=out_specs,
            scratch_shapes=scratch,
        ),
        out_shape=outs,
        compiler_params=pltpu.CompilerParams(vmem_limit_bytes=mib * MIB),
        **more,
    )(*scalars, *ins, *after)


def part_of_body(image, where_ref, part_in, share_in, out, hold, load_sems, store_sems):
    rows = out.shape[0]
    step = rows // 4
    start = (image * 2 + 1 - where_ref[0]) * rows

    def load(n):
        source = part_in.at[0, pl.ds(pl.multiple_of(start + n * step, step), step)]
        return pltpu.make_async_copy(source, hold.at[pl.ds(n * step, step)], load_sems.at[n])

    def store(n):
        at = pl.ds(n * step, step)
        return pltpu.make_async_copy(hold.at[at], out.at[at], store_sems.at[n])

    for n in range(4):
        load(n).start()
    for n in range(4):
        load(n).wait()
        store(n).start()
    for n in range(4):
        store(n).wait()


def part_of(image, where, vit_partial, vit_residual, after):
    return call(
        functools.partial(part_of_body, image),
        (1,),
        [where],
        [vit_partial, vit_residual],
        [ANYWHERE] * 2,
        shape(vit_residual.shape),
        ANYWHERE,
        scratch=[
            pltpu.VMEM(vit_residual.shape, BF),
            pltpu.SemaphoreType.DMA((4,)),
            pltpu.SemaphoreType.DMA((4,)),
        ],
        after=after,
        mib=60,
    )


def lanes(width):
    return [slice(start, start + LANES) for start in range(0, width, LANES)]


def chip_sum_body(image, where_ref, part_ref, theirs_ref, residual_ref, out_ref):
    scale = jnp.where(where_ref[1] == image, 1.0, 0.0)
    for at in lanes(out_ref.shape[1]):
        total = part_ref[0, :, at].astype(F32) + theirs_ref[:, at].astype(F32)
        out_ref[:, at] = (total + scale * residual_ref[:, at].astype(F32)).astype(BF)


def chip_sum(image, where, vit_partial, theirs, residual):
    rows, width = residual.shape
    step = rows // 4
    plain = pl.BlockSpec((step, width), lambda i, where_ref: (i, 0))
    return call(
        functools.partial(chip_sum_body, image),
        (4,),
        [where],
        [vit_partial, theirs, residual],
        [
            pl.BlockSpec(
                (1, step, width), lambda i, where_ref: (0, (image * 2 + where_ref[0]) * 4 + i, 0)
            ),
            plain,
            plain,
        ],
        shape((rows, width)),
        plain,
        cost_estimate=cost(0, 8 * rows * width),
    )


def centre_rows(first_ref, second_ref, hold_ref, rows):
    width = hold_ref.shape[1]
    total = 0.0
    for at in lanes(width):
        stream = first_ref[rows, at].astype(F32) + second_ref[rows, at].astype(F32)
        hold_ref[rows, at] = stream
        total = total + stream
    row_mean = jnp.sum(total, axis=-1, keepdims=True) * (1.0 / width)
    total = 0.0
    for at in lanes(width):
        centred = hold_ref[rows, at] - row_mean
        hold_ref[rows, at] = centred
        total = total + centred * centred
    return lax.rsqrt(jnp.sum(total, axis=-1, keepdims=True) * (1.0 / width) + 1e-06)


def norm_body(mine_ref, other_ref, gain_ref, out_ref, hold_ref):
    rows = slice(None)
    inv_std = centre_rows(mine_ref, other_ref, hold_ref, rows)
    for at in lanes(out_ref.shape[1]):
        out_ref[:, at] = (hold_ref[:, at] * inv_std * gain_ref[:, at]).astype(BF)


def norm(mine, other, gain, after):
    rows, width = mine.shape
    plain = pl.BlockSpec((rows // 4, width), lambda i: (i, 0))
    return call(
        norm_body,
        (4,),
        [],
        [mine, other, gain],
        [plain, plain, pl.BlockSpec((1, width), lambda i: (0, 0))],
        shape((rows, width)),
        plain,
        scratch=[pltpu.VMEM((rows // 4, width), F32)],
        after=after,
        cost_estimate=cost(0, 6 * rows * width),
    )


def norm_back_body(where_ref, gain_ref, *refs):
    first, second = refs[:4], refs[4:8]
    out, held, hold, result, load_sems, store_sems = refs[8:]
    width = hold.shape[1]
    rows = held.shape[1] // 4

    def loads(n, group):
        at = pl.ds(n * rows, rows)
        return [
            pltpu.make_async_copy(source.at[at], held.at[j, at], load_sems.at[j, n])
            for j, source in enumerate(group)
        ]

    for side, group in enumerate((first, second)):

        @pl.when(where_ref[1] == side)
        def _(group=group):
            for n in range(4):
                for copy in loads(n, group):
                    copy.start()

    stores = []
    for n in range(4):
        for copy in loads(n, first):
            copy.wait()
        part = slice(n * rows, (n + 1) * rows)
        inv_std = centre_rows(held.at[0], held.at[1], hold, part)
        sum_grad = sum_proj = 0.0
        for at in lanes(width):
            scaled = held[2, part, at].astype(F32) + held[3, part, at].astype(F32)
            scaled = scaled * gain_ref[:, at]
            result[part, at] = scaled
            sum_grad = sum_grad + scaled
            sum_proj = sum_proj + scaled * hold[part, at]
        mean_grad = jnp.sum(sum_grad, axis=-1, keepdims=True) * (1.0 / width)
        mean_proj = jnp.sum(sum_proj, axis=-1, keepdims=True) * inv_std * (1.0 / width)
        for at in lanes(width):
            normal_rows = hold[part, at] * inv_std
            result[part, at] = inv_std * (result[part, at] - mean_grad - normal_rows * mean_proj)
        at = pl.ds(n * rows, rows)
        stores.append(pltpu.make_async_copy(result.at[at], out.at[at], store_sems.at[n]))
        stores[n].start()
    for copy in stores:
        copy.wait()


def norm_back(where, gain, first, second):
    rows, width = first[0].shape
    return call(
        norm_back_body,
        (1,),
        [where],
        [gain, *first, *second],
        [pl.BlockSpec((1, width), lambda i, where_ref: (0, 0))] + [ANYWHERE] * 8,
        shape((rows, width), F32),
        ANYWHERE,
        scratch=[
            pltpu.VMEM((4, rows, width), BF),
            pltpu.VMEM((rows, width), F32),
            pltpu.VMEM((rows, width), F32),
            pltpu.SemaphoreType.DMA((4, 4)),
            pltpu.SemaphoreType.DMA((4,)),
        ],
        mib=56,
        cost_estimate=cost(0, 12 * rows * width),
    )


def ring_sum_body(where_ref, *refs):
    *blocks, kept_ref, sent_ref = refs
    rows = kept_ref.shape[0]

    def total(block):
        at = pl.ds(pl.multiple_of(block * rows, rows), rows)
        return sum(ref[at].astype(F32) for ref in blocks)

    sent_ref[...] = total(1 - where_ref[4]).astype(BF)
    kept_ref[...] = total(where_ref[4])


def ring_sum(where, blocks, after):
    rows, width = blocks[0].shape
    whole = pl.BlockSpec((rows, width), lambda i, where_ref: (0, 0))
    half = pl.BlockSpec((rows // 2, width), lambda i, where_ref: (0, 0))
    return call(
        ring_sum_body,
        (1,),
        [where],
        blocks,
        [whole] * len(blocks),
        [shape((rows // 2, width), F32), shape((rows // 2, width))],
        [half, half],
        after=after,
        cost_estimate=cost(0, 12 * rows * width),
    )


def last_sum_body(kept_ref, got_ref, key_ref, value_ref):
    total = kept_ref[...] + got_ref[...].astype(F32)
    width = key_ref.shape[1]
    key_ref[...] = total[:, :width]
    value_ref[...] = total[:, width:]


def last_sum(kept, got, after):
    rows, width = kept.shape
    whole = pl.BlockSpec((rows, width), lambda i: (0, 0))
    half = pl.BlockSpec((rows, width // 2), lambda i: (0, 0))
    return call(
        last_sum_body,
        (1,),
        [],
        [kept, got],
        [whole, whole],
        [shape((rows, width // 2), F32)] * 2,
        [half, half],
        after=after,
        cost_estimate=cost(0, 10 * rows * width),
    )


def strips_body(where_ref, own_in, far_in, *rest):
    outs = rest[:RING]
    own_ref, far_ref, hold, load_sems, store_sems = rest[RING:]
    total_rows, width = own_ref.shape
    step = total_rows // 4
    piece = width // (2 * RING * RING)
    refs = (own_ref, far_ref)

    def load(n, half):
        at = pl.ds(n * step, step)
        source = (own_in, far_in)[half]
        return pltpu.make_async_copy(source.at[at], refs[half].at[at], load_sems.at[half, n])

    def store(n, k):
        at = pl.ds(n * step, step)
        source = hold.at[lax.rem(where_ref[2] + k, RING)]
        return pltpu.make_async_copy(source.at[:, at], outs[k].at[:, at], store_sems.at[k, n])

    def fill(n, along_y):
        at = slice(n * step, (n + 1) * step)
        for half in range(2):
            for a in range(RING):
                for b in range(RING):
                    for x in range(2):
                        z, y = (b, a) if along_y else (a, b)
                        start = ((z * 2 + x) * RING + y) * piece
                        spot = (b * 2 + x) * piece
                        hold[a, half, at, spot : spot + piece] = refs[half][at, start : start + piece]

    for n in range(4):
        for half in range(2):
            load(n, half).start()
    for n in range(4):
        for half in range(2):
            load(n, half).wait()
        pl.when(where_ref[0] == 0)(functools.partial(fill, n, True))
        pl.when(where_ref[0] == 1)(functools.partial(fill, n, False))
        for k in range(RING):
            store(n, k).start()
    for n in range(4):
        for k in range(RING):
            store(n, k).wait()


def strips(where, own, far, after):
    rows, width = own.shape
    part = width // RING
    return call(
        strips_body,
        (1,),
        [where],
        [own, far],
        [ANYWHERE] * 2,
        [shape((2, rows, part))] * RING,
        [ANYWHERE] * RING,
        scratch=[
            pltpu.VMEM((rows, width), BF),
            pltpu.VMEM((rows, width), BF),
            pltpu.VMEM((RING, 2, rows, part), BF),
            pltpu.SemaphoreType.DMA((2, 4)),
            pltpu.SemaphoreType.DMA((RING, 4)),
        ],
        after=after,
        cost_estimate=cost(0, 8 * rows * width),
    )


def image_body(image, pick_ref, len_ref, own_in, far_in, key_in, value_in, q_in, g_in, *rest):
    context_out, query_grad_out, near_out, away_out, grads_ref = rest[-19:-14]
    rows, keys, values, total, q_ref, g_ref, context_ref, query_grad_ref, back = rest[-14:-5]
    row_sems, weight_sems, text_sems, back_sems, done_sems = rest[-5:]
    half = rows.shape[0] // 2
    chunk = keys.shape[0] // CUTS
    width = keys.shape[1]
    example = pick_ref[image]
    limit = len_ref[example]

    def at(n):
        return pl.ds(pl.multiple_of(n * chunk, chunk), chunk)

    def row_loads(n):
        return [
            pltpu.make_async_copy(own_in.at[:, at(n)], rows.at[:half, at(n)], row_sems.at[0, n]),
            pltpu.make_async_copy(far_in.at[:, at(n)], rows.at[half:, at(n)], row_sems.at[1, n]),
        ]

    def weight_loads(n):
        return [
            pltpu.make_async_copy(key_in.at[at(n)], keys.at[at(n)], weight_sems.at[0, n]),
            pltpu.make_async_copy(value_in.at[at(n)], values.at[at(n)], weight_sems.at[1, n]),
        ]

    def back_stores(n):
        return [
            pltpu.make_async_copy(back.at[:half, at(n)], near_out.at[:, at(n)], back_sems.at[0, n]),
            pltpu.make_async_copy(back.at[half:, at(n)], away_out.at[:, at(n)], back_sems.at[1, n]),
        ]

    text_loads = [
        pltpu.make_async_copy(q_in.at[example], q_ref, text_sems.at[0]),
        pltpu.make_async_copy(g_in.at[example], g_ref, text_sems.at[1]),
    ]
    text_stores = [
        pltpu.make_async_copy(context_ref, context_out.at[example], done_sems.at[0]),
        pltpu.make_async_copy(query_grad_ref, query_grad_out.at[example], done_sems.at[1]),
    ]

    @pl.loop(0, CUTS)
    def _(n):
        for copy in row_loads(n) + weight_loads(n):
            copy.start()

    for copy in text_loads:
        copy.start()
    total[...] = jnp.zeros_like(total)

    @pl.loop(0, CUTS)
    def _(n):
        for copy in row_loads(n) + weight_loads(n):
            copy.wait()
        left = rows[:, at(n)]
        total[:, :width] += dot(left, keys[at(n)])
        total[:, width:] += dot(left, values[at(n)])

    for copy in text_loads:
        copy.wait()
    mask = lax.broadcasted_iota(jnp.int32, (q_ref.shape[0], 1), 0) < limit
    for head in range(width // HD):
        key_at = slice(head * HD, (head + 1) * HD)
        value_at = slice(width + head * HD, width + (head + 1) * HD)
        key, value = total[:, key_at].astype(BF), total[:, value_at].astype(BF)
        q = q_ref[:, key_at]
        scores = dot(q, key, ((1,), (1,))) * HD ** (-0.5)
        exp_terms = jnp.exp(scores - jnp.max(scores, axis=-1, keepdims=True))
        softmax_w = exp_terms / jnp.sum(exp_terms, axis=-1, keepdims=True)
        weights_bf = softmax_w.astype(BF)
        context_ref[:, key_at] = jnp.where(mask, dot(weights_bf, value), 0.0)
        upstream = jnp.where(mask, g_ref[:, key_at].astype(F32), 0.0).astype(BF)
        weight_grad = dot(upstream, value, ((1,), (1,)))
        centre = jnp.sum(weight_grad * softmax_w, axis=-1, keepdims=True)
        score_grad = (softmax_w * (weight_grad - centre) * HD ** (-0.5)).astype(BF)
        query_grad_ref[:, key_at] = dot(score_grad, key)
        grads_ref[:, key_at] = dot(score_grad, q, ((0,), (0,))).astype(BF)
        grads_ref[:, value_at] = dot(weights_bf, upstream, ((0,), (0,))).astype(BF)
    for copy in text_stores:
        copy.start()

    @pl.loop(0, CUTS)
    def _(n):
        term = dot(grads_ref[:, :width], keys[at(n)], ((1,), (1,)))
        term = term + dot(grads_ref[:, width:], values[at(n)], ((1,), (1,)))
        back[:, at(n)] = term.astype(BF)
        for copy in back_stores(n):
            copy.start()

    @pl.loop(0, CUTS)
    def _(n):
        for copy in back_stores(n):
            copy.wait()

    for copy in text_stores:
        copy.wait()


def image_step(
    image, pick, text_len, own, far, key_weight, value_weight, queries, context_grad, partly, after
):
    text_rows, width = queries.shape[1:]
    half, depth = own.shape
    flat = (2 * half, 2 * width)
    sems = pltpu.SemaphoreType.DMA
    return call(
        functools.partial(image_body, image),
        (1,),
        [pick, text_len],
        [own, far, key_weight, value_weight, queries, context_grad, *partly],
        [ANYWHERE] * (6 + len(partly)),
        [shape(queries.shape, F32)] * 2 + [shape(own.shape)] * 2 + [shape(flat)],
        [ANYWHERE] * 4 + [pl.BlockSpec(flat, lambda i, *scalars: (0, 0))],
        scratch=[
            pltpu.VMEM((2 * half, depth), BF),
            pltpu.VMEM(key_weight.shape, BF),
            pltpu.VMEM(key_weight.shape, BF),
            pltpu.VMEM(flat, F32),
            pltpu.VMEM((text_rows, width), BF),
            pltpu.VMEM((text_rows, width), BF),
            pltpu.VMEM((text_rows, width), F32),
            pltpu.VMEM((text_rows, width), F32),
            pltpu.VMEM((2 * half, depth), BF),
            sems((2, CUTS)),
            sems((2, CUTS)),
            sems((2,)),
            sems((2, CUTS)),
            sems((2,)),
        ],
        after=after,
        input_output_aliases={8: 0, 9: 1} if partly else {},
        mib=44,
        cost_estimate=cost(
            16 * half * depth * width + 24 * text_rows * half * width,
            4 * depth * (2 * half + width) + 12 * text_rows * width,
            2 * text_rows * half * width // HD,
        ),
    )


def weight_grad_body(first, pieces, where_ref, *refs):
    lefts_in, rights_in, rest = refs[:RING], refs[RING : RING + pieces], refs[RING + pieces :]
    left, right, result, left_sems, right_sems, store_sems = rest[-6:]
    outs = rest[:1] if first else rest[1:-6]
    rows = right.shape[0] // RING
    chunk, width = result.shape[1:]
    half = rows // 2
    wide = width // 2

    def right_loads():
        start = 0
        for k, source in enumerate(rights_in):
            target = right.at[pl.ds(start, source.shape[0])]
            start += source.shape[0]
            yield pltpu.make_async_copy(source, target, right_sems.at[k])

    def left_load(n, k, h):
        columns = pl.ds(pl.multiple_of(lax.rem(where_ref[3] + n, RING) * chunk, chunk), chunk)
        at = pl.ds(k * rows + h * half, half)
        source = lefts_in[k].at[h, :, columns]
        return pltpu.make_async_copy(source, left.at[n, at], left_sems.at[n, k, h])

    def stores(n):
        if first:
            return [pltpu.make_async_copy(result.at[n], outs[0].at[n], store_sems.at[n])]
        if n != 2:
            target = outs[(0, 1, None, 4)[n]]
            return [pltpu.make_async_copy(result.at[n], target, store_sems.at[n])]
        cut = chunk // 2
        top, bottom = pl.ds(0, cut), pl.ds(cut, cut)
        return [
            pltpu.make_async_copy(result.at[n, top], outs[2], store_sems.at[n]),
            pltpu.make_async_copy(result.at[n, bottom], outs[3], store_sems.at[RING]),
        ]

    each = [(k, h) for k in range(RING) for h in range(2)]
    order = (2, 1, 3, 0)
    for copy in right_loads():
        copy.start()
    for n in order:
        for k, h in each:
            left_load(n, k, h).start()
    for copy in right_loads():
        copy.wait()
    for n in order:
        for k, h in each:
            left_load(n, k, h).wait()
        for columns in (slice(0, wide), slice(wide, width)):
            total = dot(left[n], right[:, columns], ((0,), (0,)))
            if not first:
                total = total + rest[0][n, :, columns].astype(F32)
            result[n, :, columns] = total.astype(BF)
        for copy in stores(n):
            copy.start()
    for n in order:
        for copy in stores(n):
            copy.wait()


def weight_grad(where, lefts, rights, so_far=None, after=()):
    halves, rows, part = lefts[0].shape
    width = rights[0].shape[1]
    chunk, pieces = part // RING, len(rights)
    first = so_far is None
    whole = (RING, chunk, width)
    heights = [chunk, chunk, chunk // 2, chunk // 2, chunk]
    outs = [shape(whole)] if first else [shape((height, width)) for height in heights]
    return call(
        functools.partial(weight_grad_body, first, pieces),
        (1,),
        [where],
        [*lefts, *rights] + ([] if first else [so_far]),
        [ANYWHERE] * (RING + pieces)
        + ([] if first else [pl.BlockSpec(whole, lambda i, where_ref: (0, 0, 0))]),
        outs,
        [ANYWHERE] * len(outs),
        scratch=[
            pltpu.VMEM((RING, RING * halves * rows, chunk), BF),
            pltpu.VMEM((RING * halves * rows, width), BF),
            pltpu.VMEM(whole, BF),
            pltpu.SemaphoreType.DMA((RING, RING, 2)),
            pltpu.SemaphoreType.DMA((pieces,)),
            pltpu.SemaphoreType.DMA((RING + 1,)),
        ],
        after=after,
        cost_estimate=cost(0, 0),
        mib=56 if first else 20,
    )


def relay_body(up_ref, got_up_ref, down_ref, got_down_ref, up_out, down_out):
    cut = got_up_ref.shape[0]
    up_out[:cut] = (up_ref[:cut].astype(F32) + got_up_ref[...].astype(F32)).astype(BF)
    up_out[cut:] = up_ref[cut:]
    down_out[:cut] = down_ref[:cut]
    down_out[cut:] = (down_ref[cut:].astype(F32) + got_down_ref[...].astype(F32)).astype(BF)


def relay(up, got_up, down, got_down):
    whole = pl.BlockSpec(up.shape, lambda i: (0, 0))
    half = pl.BlockSpec(got_up.shape, lambda i: (0, 0))
    return call(
        relay_body,
        (1,),
        [],
        [up, got_up, down, got_down],
        [whole, half, whole, half],
        [shape(up.shape)] * 2,
        [whole, whole],
        cost_estimate=cost(0, 0),
    )


def later(array, after):
    return call(
        lambda *refs: None,
        (1,),
        [],
        [array],
        [ANYWHERE],
        shape(array.shape, array.dtype),
        ANYWHERE,
        after=after,
        input_output_aliases={0: 0},
    )


def hop(first, distance):
    pairs = []
    for z in range(RING):
        for y in range(RING):
            for core in range(2):
                along_y = (core == 0) == first
                to = (z, (y + distance) % RING) if along_y else ((z + distance) % RING, y)
                pairs.append(((z * RING + y) * 2 + core, (to[0] * RING + to[1]) * 2 + core))
    return pairs


def rotate(array, first, distance):
    return lax.ppermute(array, ("z", "y", "c"), hop(first, distance))


def local(
    vit_partial,
    vit_residual,
    ln_gain,
    key_weight,
    value_weight,
    queries,
    context_grad,
    text_len,
    image_pick,
):
    share, model_width = vit_residual.shape
    width = key_weight.shape[1]
    core, side, cross = lax.axis_index("c"), lax.axis_index("xl"), lax.axis_index("xh")
    y, z = lax.axis_index("y"), lax.axis_index("z")
    where = jnp.stack([core, side, jnp.where(core == 0, y, z), jnp.where(core == 0, z, y), cross])
    pick = image_pick[0]
    gain = ln_gain[None, :]

    mine, other, after = [], [], []
    for image in range(2):
        sent = part_of(image, where, vit_partial, vit_residual, after)
        after = [sent]
        theirs = lax.ppermute(sent, "c", SWAP)
        mine.append(chip_sum(image, where, vit_partial, theirs, vit_residual))
        other.append(lax.ppermute(mine[image], "xl", SWAP))

    def spread(array, firsts):
        return [array] + [rotate(firsts[k], True, k) for k in range(1, RING)]

    def gather(array):
        half = array.shape[0] // 2
        below, above = rotate(array, True, 1), rotate(array, True, RING - 1)
        top = rotate(below[:half], True, 1)
        bottom = rotate(above[half:], True, RING - 1)
        return [array, below, top, bottom, above]

    def core_sum(near_rows, away_rows):
        theirs = lax.ppermute(away_rows, "c", SWAP)
        return (near_rows.astype(F32) + theirs.astype(F32)).astype(BF)

    def step(image, own, far, texts, after):
        given = (key_weight, value_weight, queries, context_grad)
        return image_step(image, pick, text_len, own, far, *given, texts, after)

    own = norm(mine[0], other[0], gain, [mine[1]])
    far = lax.ppermute(own, "c", SWAP)
    pieces = strips(where, own, far, [])
    lefts = spread(pieces[0], pieces)
    *texts, near_rows, away_rows, grads = step(0, own, far, [], [pieces[0]])
    grads = later(grads, lefts[1:])
    rights = spread(grads, [grads] * RING)

    own = norm(mine[1], other[1], gain, [near_rows, *rights[1:]])
    far = lax.ppermute(own, "c", SWAP)
    pieces = strips(where, own, far, [])
    last_lefts = spread(pieces[0], pieces)
    near_0, away_0 = near_rows, away_rows
    *texts, near_rows, away_rows, grads = step(1, own, far, texts, [pieces[0]])
    share_0 = core_sum(near_0, later(away_0, [pieces[0]]))
    (so_far,) = weight_grad(where, lefts, rights, after=[near_rows, share_0])
    grads = later(grads, last_lefts[1:] + [so_far])
    last_rights = gather(grads)
    share_1 = core_sum(near_rows, later(away_rows, [grads]))

    from_second = lax.ppermute(share_0, "xl", [(1, 0)])
    from_first = lax.ppermute(share_1, "xl", [(0, 1)])
    blocks = weight_grad(where, last_lefts, last_rights, so_far, [share_0, share_1])
    kept, up, across_up, across_down, down = blocks
    got_up = rotate(across_up, False, 1)
    got_down = rotate(across_down, False, RING - 1)
    up, down = relay(up, got_up, down, got_down)
    got = [rotate(up, False, 1), rotate(down, False, RING - 1)]
    stream_grad = norm_back(
        where,
        gain,
        [mine[0], other[0], share_0, from_second],
        [mine[1], other[1], share_1, from_first],
    )
    kept, sent = ring_sum(where, [kept, *got], [from_first, from_second])
    got = lax.ppermute(sent, "xh", SWAP)
    key_weight_grad, value_weight_grad = last_sum(kept, got, [stream_grad])
    return texts[0], texts[1], key_weight_grad, value_weight_grad, stream_grad


def solution(mesh):
    fine = Mesh(mesh.devices.reshape(4, 2, 4, 2, 2), ("z", "xh", "y", "xl", "c"))
    dp, mp = ("z", "xh", "y"), ("xl", "c")
    placed = (
        P(mp, dp, None),
        P(dp + mp, None),
        P(),
        P(None, mp),
        P(None, mp),
        P(dp, None, mp),
        P(dp, None, mp),
        P(dp),
        P(dp, None),
    )
    return jax.shard_map(
        local,
        mesh=fine,
        in_specs=placed,
        out_specs=(P(dp, None, mp), P(dp, None, mp), P(dp, mp), P(dp, mp), P(dp + mp, None)),
        check_vma=False,
    )
```

```python
import functools

import jax
import jax.numpy as jnp
from jax import lax
from jax.experimental import pallas as pl
from jax.experimental.pallas import tpu as pltpu
from jax.sharding import Mesh, PartitionSpec as P

HD = 256
RING = 4
BF = jnp.bfloat16
F32 = jnp.float32
SWAP = [(0, 1), (1, 0)]
MIB = 1024 * 1024
LANES = 512
CUTS = 4
ANYWHERE = pl.BlockSpec(memory_space=pl.ANY)


def dot(left, right, dims=((1,), (0,))):
    return lax.dot_general(left, right, (dims, ((), ())), preferred_element_type=F32)


def shape(dims, kind=BF):
    return jax.ShapeDtypeStruct(dims, kind)


def cost(flops, moved, special=0):
    return pl.CostEstimate(flops=flops, bytes_accessed=moved, transcendentals=special)


def call(body, grid, scalars, ins, in_specs, outs, out_specs, scratch=(), after=(), mib=20, **more):
    count, waits = len(scalars) + len(ins), len(after)

    def with_waits(*refs):
        body(*refs[:count], *refs[count + waits :])

    return pl.pallas_call(
        with_waits,
        grid_spec=pltpu.PrefetchScalarGridSpec(
            num_scalar_prefetch=len(scalars),
            grid=grid,
            in_specs=list(in_specs) + [ANYWHERE] * waits,
            out_specs=out_specs,
            scratch_shapes=scratch,
        ),
        out_shape=outs,
        compiler_params=pltpu.CompilerParams(vmem_limit_bytes=mib * MIB),
        **more,
    )(*scalars, *ins, *after)


def part_of_body(image, where_ref, part_in, share_in, out, hold, load_sems, store_sems):
    rows = out.shape[0]
    step = rows // 4
    start = (image * 2 + 1 - where_ref[0]) * rows

    def load(n):
        source = part_in.at[0, pl.ds(pl.multiple_of(start + n * step, step), step)]
        return pltpu.make_async_copy(source, hold.at[pl.ds(n * step, step)], load_sems.at[n])

    def store(n):
        at = pl.ds(n * step, step)
        return pltpu.make_async_copy(hold.at[at], out.at[at], store_sems.at[n])

    for n in range(4):
        load(n).start()
    for n in range(4):
        load(n).wait()
        store(n).start()
    for n in range(4):
        store(n).wait()


def part_of(image, where, vit_partial, vit_residual, after):
    return call(
        functools.partial(part_of_body, image),
        (1,),
        [where],
        [vit_partial, vit_residual],
        [ANYWHERE] * 2,
        shape(vit_residual.shape),
        ANYWHERE,
        scratch=[
            pltpu.VMEM(vit_residual.shape, BF),
            pltpu.SemaphoreType.DMA((4,)),
            pltpu.SemaphoreType.DMA((4,)),
        ],
        after=after,
        mib=60,
    )


def lanes(width):
    return [slice(start, start + LANES) for start in range(0, width, LANES)]


def chip_sum_body(image, where_ref, part_ref, theirs_ref, residual_ref, out_ref):
    scale = jnp.where(where_ref[1] == image, 1.0, 0.0)
    for at in lanes(out_ref.shape[1]):
        total = part_ref[0, :, at].astype(F32) + theirs_ref[:, at].astype(F32)
        out_ref[:, at] = (total + scale * residual_ref[:, at].astype(F32)).astype(BF)


def chip_sum(image, where, vit_partial, theirs, residual):
    rows, width = residual.shape
    step = rows // 4
    plain = pl.BlockSpec((step, width), lambda i, where_ref: (i, 0))
    return call(
        functools.partial(chip_sum_body, image),
        (4,),
        [where],
        [vit_partial, theirs, residual],
        [
            pl.BlockSpec(
                (1, step, width), lambda i, where_ref: (0, (image * 2 + where_ref[0]) * 4 + i, 0)
            ),
            plain,
            plain,
        ],
        shape((rows, width)),
        plain,
        cost_estimate=cost(0, 8 * rows * width),
    )


def centre_rows(first_ref, second_ref, hold_ref, rows):
    width = hold_ref.shape[1]
    total = 0.0
    for at in lanes(width):
        stream = first_ref[rows, at].astype(F32) + second_ref[rows, at].astype(F32)
        hold_ref[rows, at] = stream
        total = total + stream
    row_mean = jnp.sum(total, axis=-1, keepdims=True) * (1.0 / width)
    total = 0.0
    for at in lanes(width):
        centred = hold_ref[rows, at] - row_mean
        hold_ref[rows, at] = centred
        total = total + centred * centred
    return lax.rsqrt(jnp.sum(total, axis=-1, keepdims=True) * (1.0 / width) + 1e-06)


def norm_body(mine_ref, other_ref, gain_ref, out_ref, hold_ref):
    rows = slice(None)
    inv_std = centre_rows(mine_ref, other_ref, hold_ref, rows)
    for at in lanes(out_ref.shape[1]):
        out_ref[:, at] = (hold_ref[:, at] * inv_std * gain_ref[:, at]).astype(BF)


def norm(mine, other, gain, after):
    rows, width = mine.shape
    plain = pl.BlockSpec((rows // 4, width), lambda i: (i, 0))
    return call(
        norm_body,
        (4,),
        [],
        [mine, other, gain],
        [plain, plain, pl.BlockSpec((1, width), lambda i: (0, 0))],
        shape((rows, width)),
        plain,
        scratch=[pltpu.VMEM((rows // 4, width), F32)],
        after=after,
        cost_estimate=cost(0, 6 * rows * width),
    )


def norm_back_body(where_ref, gain_ref, *refs):
    first, second = refs[:4], refs[4:8]
    out, held, hold, result, load_sems, store_sems = refs[8:]
    width = hold.shape[1]
    rows = held.shape[1] // 4

    def loads(n, group):
        at = pl.ds(n * rows, rows)
        return [
            pltpu.make_async_copy(source.at[at], held.at[j, at], load_sems.at[j, n])
            for j, source in enumerate(group)
        ]

    for side, group in enumerate((first, second)):

        @pl.when(where_ref[1] == side)
        def _(group=group):
            for n in range(4):
                for copy in loads(n, group):
                    copy.start()

    stores = []
    for n in range(4):
        for copy in loads(n, first):
            copy.wait()
        part = slice(n * rows, (n + 1) * rows)
        inv_std = centre_rows(held.at[0], held.at[1], hold, part)
        sum_grad = sum_proj = 0.0
        for at in lanes(width):
            scaled = held[2, part, at].astype(F32) + held[3, part, at].astype(F32)
            scaled = scaled * gain_ref[:, at]
            result[part, at] = scaled
            sum_grad = sum_grad + scaled
            sum_proj = sum_proj + scaled * hold[part, at]
        mean_grad = jnp.sum(sum_grad, axis=-1, keepdims=True) * (1.0 / width)
        mean_proj = jnp.sum(sum_proj, axis=-1, keepdims=True) * inv_std * (1.0 / width)
        for at in lanes(width):
            normal_rows = hold[part, at] * inv_std
            result[part, at] = inv_std * (result[part, at] - mean_grad - normal_rows * mean_proj)
        at = pl.ds(n * rows, rows)
        stores.append(pltpu.make_async_copy(result.at[at], out.at[at], store_sems.at[n]))
        stores[n].start()
    for copy in stores:
        copy.wait()


def norm_back(where, gain, first, second):
    rows, width = first[0].shape
    return call(
        norm_back_body,
        (1,),
        [where],
        [gain, *first, *second],
        [pl.BlockSpec((1, width), lambda i, where_ref: (0, 0))] + [ANYWHERE] * 8,
        shape((rows, width), F32),
        ANYWHERE,
        scratch=[
            pltpu.VMEM((4, rows, width), BF),
            pltpu.VMEM((rows, width), F32),
            pltpu.VMEM((rows, width), F32),
            pltpu.SemaphoreType.DMA((4, 4)),
            pltpu.SemaphoreType.DMA((4,)),
        ],
        mib=56,
        cost_estimate=cost(0, 12 * rows * width),
    )


def ring_sum_body(where_ref, *refs):
    *blocks, kept_ref, sent_ref = refs
    rows = kept_ref.shape[0]

    def total(block):
        at = pl.ds(pl.multiple_of(block * rows, rows), rows)
        return sum(ref[at].astype(F32) for ref in blocks)

    sent_ref[...] = total(1 - where_ref[4]).astype(BF)
    kept_ref[...] = total(where_ref[4])


def ring_sum(where, blocks, after):
    rows, width = blocks[0].shape
    whole = pl.BlockSpec((rows, width), lambda i, where_ref: (0, 0))
    half = pl.BlockSpec((rows // 2, width), lambda i, where_ref: (0, 0))
    return call(
        ring_sum_body,
        (1,),
        [where],
        blocks,
        [whole] * len(blocks),
        [shape((rows // 2, width), F32), shape((rows // 2, width))],
        [half, half],
        after=after,
        cost_estimate=cost(0, 12 * rows * width),
    )


def last_sum_body(kept_ref, got_ref, key_ref, value_ref):
    total = kept_ref[...] + got_ref[...].astype(F32)
    width = key_ref.shape[1]
    key_ref[...] = total[:, :width]
    value_ref[...] = total[:, width:]


def last_sum(kept, got, after):
    rows, width = kept.shape
    whole = pl.BlockSpec((rows, width), lambda i: (0, 0))
    half = pl.BlockSpec((rows, width // 2), lambda i: (0, 0))
    return call(
        last_sum_body,
        (1,),
        [],
        [kept, got],
        [whole, whole],
        [shape((rows, width // 2), F32)] * 2,
        [half, half],
        after=after,
        cost_estimate=cost(0, 10 * rows * width),
    )


def strips_body(where_ref, own_in, far_in, *rest):
    outs = rest[:RING]
    own_ref, far_ref, hold, load_sems, store_sems = rest[RING:]
    total_rows, width = own_ref.shape
    step = total_rows // 4
    piece = width // (2 * RING * RING)
    refs = (own_ref, far_ref)

    def load(n, half):
        at = pl.ds(n * step, step)
        source = (own_in, far_in)[half]
        return pltpu.make_async_copy(source.at[at], refs[half].at[at], load_sems.at[half, n])

    def store(n, k):
        at = pl.ds(n * step, step)
        source = hold.at[lax.rem(where_ref[2] + k, RING)]
        return pltpu.make_async_copy(source.at[:, at], outs[k].at[:, at], store_sems.at[k, n])

    def fill(n, along_y):
        at = slice(n * step, (n + 1) * step)
        for half in range(2):
            for a in range(RING):
                for b in range(RING):
                    for x in range(2):
                        z, y = (b, a) if along_y else (a, b)
                        start = ((z * 2 + x) * RING + y) * piece
                        spot = (b * 2 + x) * piece
                        hold[a, half, at, spot : spot + piece] = refs[half][at, start : start + piece]

    for n in range(4):
        for half in range(2):
            load(n, half).start()
    for n in range(4):
        for half in range(2):
            load(n, half).wait()
        pl.when(where_ref[0] == 0)(functools.partial(fill, n, True))
        pl.when(where_ref[0] == 1)(functools.partial(fill, n, False))
        for k in range(RING):
            store(n, k).start()
    for n in range(4):
        for k in range(RING):
            store(n, k).wait()


def strips(where, own, far, after):
    rows, width = own.shape
    part = width // RING
    return call(
        strips_body,
        (1,),
        [where],
        [own, far],
        [ANYWHERE] * 2,
        [shape((2, rows, part))] * RING,
        [ANYWHERE] * RING,
        scratch=[
            pltpu.VMEM((rows, width), BF),
            pltpu.VMEM((rows, width), BF),
            pltpu.VMEM((RING, 2, rows, part), BF),
            pltpu.SemaphoreType.DMA((2, 4)),
            pltpu.SemaphoreType.DMA((RING, 4)),
        ],
        after=after,
        cost_estimate=cost(0, 8 * rows * width),
    )


def image_body(image, pick_ref, len_ref, own_in, far_in, key_in, value_in, q_in, g_in, *rest):
    context_out, query_grad_out, near_out, away_out, grads_ref = rest[-19:-14]
    rows, keys, values, total, q_ref, g_ref, context_ref, query_grad_ref, back = rest[-14:-5]
    row_sems, weight_sems, text_sems, back_sems, done_sems = rest[-5:]
    half = rows.shape[0] // 2
    chunk = keys.shape[0] // CUTS
    width = keys.shape[1]
    example = pick_ref[image]
    limit = len_ref[example]

    def at(n):
        return pl.ds(pl.multiple_of(n * chunk, chunk), chunk)

    def row_loads(n):
        return [
            pltpu.make_async_copy(own_in.at[:, at(n)], rows.at[:half, at(n)], row_sems.at[0, n]),
            pltpu.make_async_copy(far_in.at[:, at(n)], rows.at[half:, at(n)], row_sems.at[1, n]),
        ]

    def weight_loads(n):
        return [
            pltpu.make_async_copy(key_in.at[at(n)], keys.at[at(n)], weight_sems.at[0, n]),
            pltpu.make_async_copy(value_in.at[at(n)], values.at[at(n)], weight_sems.at[1, n]),
        ]

    def back_stores(n):
        return [
            pltpu.make_async_copy(back.at[:half, at(n)], near_out.at[:, at(n)], back_sems.at[0, n]),
            pltpu.make_async_copy(back.at[half:, at(n)], away_out.at[:, at(n)], back_sems.at[1, n]),
        ]

    text_loads = [
        pltpu.make_async_copy(q_in.at[example], q_ref, text_sems.at[0]),
        pltpu.make_async_copy(g_in.at[example], g_ref, text_sems.at[1]),
    ]
    text_stores = [
        pltpu.make_async_copy(context_ref, context_out.at[example], done_sems.at[0]),
        pltpu.make_async_copy(query_grad_ref, query_grad_out.at[example], done_sems.at[1]),
    ]

    @pl.loop(0, CUTS)
    def _(n):
        for copy in row_loads(n) + weight_loads(n):
            copy.start()

    for copy in text_loads:
        copy.start()
    total[...] = jnp.zeros_like(total)

    @pl.loop(0, CUTS)
    def _(n):
        for copy in row_loads(n) + weight_loads(n):
            copy.wait()
        left = rows[:, at(n)]
        total[:, :width] += dot(left, keys[at(n)])
        total[:, width:] += dot(left, values[at(n)])

    for copy in text_loads:
        copy.wait()
    mask = lax.broadcasted_iota(jnp.int32, (q_ref.shape[0], 1), 0) < limit
    for head in range(width // HD):
        key_at = slice(head * HD, (head + 1) * HD)
        value_at = slice(width + head * HD, width + (head + 1) * HD)
        key, value = total[:, key_at].astype(BF), total[:, value_at].astype(BF)
        q = q_ref[:, key_at]
        scores = dot(q, key, ((1,), (1,))) * HD ** (-0.5)
        exp_terms = jnp.exp(scores - jnp.max(scores, axis=-1, keepdims=True))
        softmax_w = exp_terms / jnp.sum(exp_terms, axis=-1, keepdims=True)
        weights_bf = softmax_w.astype(BF)
        context_ref[:, key_at] = jnp.where(mask, dot(weights_bf, value), 0.0)
        upstream = jnp.where(mask, g_ref[:, key_at].astype(F32), 0.0).astype(BF)
        weight_grad = dot(upstream, value, ((1,), (1,)))
        centre = jnp.sum(weight_grad * softmax_w, axis=-1, keepdims=True)
        score_grad = (softmax_w * (weight_grad - centre) * HD ** (-0.5)).astype(BF)
        query_grad_ref[:, key_at] = dot(score_grad, key)
        grads_ref[:, key_at] = dot(score_grad, q, ((0,), (0,))).astype(BF)
        grads_ref[:, value_at] = dot(weights_bf, upstream, ((0,), (0,))).astype(BF)
    for copy in text_stores:
        copy.start()

    @pl.loop(0, CUTS)
    def _(n):
        term = dot(grads_ref[:, :width], keys[at(n)], ((1,), (1,)))
        term = term + dot(grads_ref[:, width:], values[at(n)], ((1,), (1,)))
        back[:, at(n)] = term.astype(BF)
        for copy in back_stores(n):
            copy.start()

    @pl.loop(0, CUTS)
    def _(n):
        for copy in back_stores(n):
            copy.wait()

    for copy in text_stores:
        copy.wait()


def image_step(
    image, pick, text_len, own, far, key_weight, value_weight, queries, context_grad, partly, after
):
    text_rows, width = queries.shape[1:]
    half, depth = own.shape
    flat = (2 * half, 2 * width)
    sems = pltpu.SemaphoreType.DMA
    return call(
        functools.partial(image_body, image),
        (1,),
        [pick, text_len],
        [own, far, key_weight, value_weight, queries, context_grad, *partly],
        [ANYWHERE] * (6 + len(partly)),
        [shape(queries.shape, F32)] * 2 + [shape(own.shape)] * 2 + [shape(flat)],
        [ANYWHERE] * 4 + [pl.BlockSpec(flat, lambda i, *scalars: (0, 0))],
        scratch=[
            pltpu.VMEM((2 * half, depth), BF),
            pltpu.VMEM(key_weight.shape, BF),
            pltpu.VMEM(key_weight.shape, BF),
            pltpu.VMEM(flat, F32),
            pltpu.VMEM((text_rows, width), BF),
            pltpu.VMEM((text_rows, width), BF),
            pltpu.VMEM((text_rows, width), F32),
            pltpu.VMEM((text_rows, width), F32),
            pltpu.VMEM((2 * half, depth), BF),
            sems((2, CUTS)),
            sems((2, CUTS)),
            sems((2,)),
            sems((2, CUTS)),
            sems((2,)),
        ],
        after=after,
        input_output_aliases={8: 0, 9: 1} if partly else {},
        mib=44,
        cost_estimate=cost(
            16 * half * depth * width + 24 * text_rows * half * width,
            4 * depth * (2 * half + width) + 12 * text_rows * width,
            2 * text_rows * half * width // HD,
        ),
    )


def weight_grad_body(first, pieces, where_ref, *refs):
    lefts_in, rights_in, rest = refs[:RING], refs[RING : RING + pieces], refs[RING + pieces :]
    left, right, result, left_sems, right_sems, store_sems = rest[-6:]
    outs = rest[:1] if first else rest[1:-6]
    rows = right.shape[0] // RING
    chunk, width = result.shape[1:]
    half = rows // 2
    wide = width // 2

    def right_loads():
        start = 0
        for k, source in enumerate(rights_in):
            target = right.at[pl.ds(start, source.shape[0])]
            start += source.shape[0]
            yield pltpu.make_async_copy(source, target, right_sems.at[k])

    def left_load(n, k, h):
        columns = pl.ds(pl.multiple_of(lax.rem(where_ref[3] + n, RING) * chunk, chunk), chunk)
        at = pl.ds(k * rows + h * half, half)
        source = lefts_in[k].at[h, :, columns]
        return pltpu.make_async_copy(source, left.at[n, at], left_sems.at[n, k, h])

    def stores(n):
        if first:
            return [pltpu.make_async_copy(result.at[n], outs[0].at[n], store_sems.at[n])]
        if n != 2:
            target = outs[(0, 1, None, 4)[n]]
            return [pltpu.make_async_copy(result.at[n], target, store_sems.at[n])]
        cut = chunk // 2
        top, bottom = pl.ds(0, cut), pl.ds(cut, cut)
        return [
            pltpu.make_async_copy(result.at[n, top], outs[2], store_sems.at[n]),
            pltpu.make_async_copy(result.at[n, bottom], outs[3], store_sems.at[RING]),
        ]

    each = [(k, h) for k in range(RING) for h in range(2)]
    order = (2, 1, 3, 0)
    for copy in right_loads():
        copy.start()
    for n in order:
        for k, h in each:
            left_load(n, k, h).start()
    for copy in right_loads():
        copy.wait()
    for n in order:
        for k, h in each:
            left_load(n, k, h).wait()
        for columns in (slice(0, wide), slice(wide, width)):
            total = dot(left[n], right[:, columns], ((0,), (0,)))
            if not first:
                total = total + rest[0][n, :, columns].astype(F32)
            result[n, :, columns] = total.astype(BF)
        for copy in stores(n):
            copy.start()
    for n in order:
        for copy in stores(n):
            copy.wait()


def weight_grad(where, lefts, rights, so_far=None, after=()):
    halves, rows, part = lefts[0].shape
    width = rights[0].shape[1]
    chunk, pieces = part // RING, len(rights)
    first = so_far is None
    whole = (RING, chunk, width)
    heights = [chunk, chunk, chunk // 2, chunk // 2, chunk]
    outs = [shape(whole)] if first else [shape((height, width)) for height in heights]
    return call(
        functools.partial(weight_grad_body, first, pieces),
        (1,),
        [where],
        [*lefts, *rights] + ([] if first else [so_far]),
        [ANYWHERE] * (RING + pieces)
        + ([] if first else [pl.BlockSpec(whole, lambda i, where_ref: (0, 0, 0))]),
        outs,
        [ANYWHERE] * len(outs),
        scratch=[
            pltpu.VMEM((RING, RING * halves * rows, chunk), BF),
            pltpu.VMEM((RING * halves * rows, width), BF),
            pltpu.VMEM(whole, BF),
            pltpu.SemaphoreType.DMA((RING, RING, 2)),
            pltpu.SemaphoreType.DMA((pieces,)),
            pltpu.SemaphoreType.DMA((RING + 1,)),
        ],
        after=after,
        cost_estimate=cost(0, 0),
    )


def relay_body(up_ref, got_up_ref, down_ref, got_down_ref, up_out, down_out):
    cut = got_up_ref.shape[0]
    up_out[:cut] = (up_ref[:cut].astype(F32) + got_up_ref[...].astype(F32)).astype(BF)
    up_out[cut:] = up_ref[cut:]
    down_out[:cut] = down_ref[:cut]
    down_out[cut:] = (down_ref[cut:].astype(F32) + got_down_ref[...].astype(F32)).astype(BF)


def relay(up, got_up, down, got_down):
    whole = pl.BlockSpec(up.shape, lambda i: (0, 0))
    half = pl.BlockSpec(got_up.shape, lambda i: (0, 0))
    return call(
        relay_body,
        (1,),
        [],
        [up, got_up, down, got_down],
        [whole, half, whole, half],
        [shape(up.shape)] * 2,
        [whole, whole],
        cost_estimate=cost(0, 0),
    )


def later(array, after):
    return call(
        lambda *refs: None,
        (1,),
        [],
        [array],
        [ANYWHERE],
        shape(array.shape, array.dtype),
        ANYWHERE,
        after=after,
        input_output_aliases={0: 0},
    )


def hop(first, distance):
    pairs = []
    for z in range(RING):
        for y in range(RING):
            for core in range(2):
                along_y = (core == 0) == first
                to = (z, (y + distance) % RING) if along_y else ((z + distance) % RING, y)
                pairs.append(((z * RING + y) * 2 + core, (to[0] * RING + to[1]) * 2 + core))
    return pairs


def rotate(array, first, distance):
    return lax.ppermute(array, ("z", "y", "c"), hop(first, distance))


def local(
    vit_partial,
    vit_residual,
    ln_gain,
    key_weight,
    value_weight,
    queries,
    context_grad,
    text_len,
    image_pick,
):
    share, model_width = vit_residual.shape
    width = key_weight.shape[1]
    core, side, cross = lax.axis_index("c"), lax.axis_index("xl"), lax.axis_index("xh")
    y, z = lax.axis_index("y"), lax.axis_index("z")
    where = jnp.stack([core, side, jnp.where(core == 0, y, z), jnp.where(core == 0, z, y), cross])
    pick = image_pick[0]
    gain = ln_gain[None, :]

    mine, other, after = [], [], []
    for image in range(2):
        sent = part_of(image, where, vit_partial, vit_residual, after)
        after = [sent]
        theirs = lax.ppermute(sent, "c", SWAP)
        mine.append(chip_sum(image, where, vit_partial, theirs, vit_residual))
        other.append(lax.ppermute(mine[image], "xl", SWAP))

    def spread(array, firsts):
        return [array] + [rotate(firsts[k], True, k) for k in range(1, RING)]

    def core_sum(near_rows, away_rows):
        theirs = lax.ppermute(away_rows, "c", SWAP)
        return (near_rows.astype(F32) + theirs.astype(F32)).astype(BF)

    def step(image, own, far, texts, after):
        given = (key_weight, value_weight, queries, context_grad)
        return image_step(image, pick, text_len, own, far, *given, texts, after)

    own = norm(mine[0], other[0], gain, [mine[1]])
    far = lax.ppermute(own, "c", SWAP)
    pieces = strips(where, own, far, [])
    lefts = spread(pieces[0], pieces)
    *texts, near_rows, away_rows, grads = step(0, own, far, [], [pieces[0]])
    grads = later(grads, lefts[1:])
    rights = spread(grads, [grads] * RING)

    own = norm(mine[1], other[1], gain, [near_rows, *rights[1:]])
    far = lax.ppermute(own, "c", SWAP)
    pieces = strips(where, own, far, [])
    last_lefts = spread(pieces[0], pieces)
    near_0, away_0 = near_rows, away_rows
    *texts, near_rows, away_rows, grads = step(1, own, far, texts, [pieces[0]])
    share_0 = core_sum(near_0, later(away_0, [pieces[0]]))
    grads = later(grads, last_lefts[1:])
    last_rights = spread(grads, [grads] * RING)
    (so_far,) = weight_grad(where, lefts, rights, after=[grads, share_0])
    share_1 = core_sum(near_rows, later(away_rows, [grads]))

    from_second = lax.ppermute(share_0, "xl", [(1, 0)])
    from_first = lax.ppermute(share_1, "xl", [(0, 1)])
    blocks = weight_grad(where, last_lefts, last_rights, so_far, [share_0, share_1])
    kept, up, across_up, across_down, down = blocks
    got_up = rotate(across_up, False, 1)
    got_down = rotate(across_down, False, RING - 1)
    up, down = relay(up, got_up, down, got_down)
    got = [rotate(up, False, 1), rotate(down, False, RING - 1)]
    stream_grad = norm_back(
        where,
        gain,
        [mine[0], other[0], share_0, from_second],
        [mine[1], other[1], share_1, from_first],
    )
    kept, sent = ring_sum(where, [kept, *got], [from_first, from_second])
    got = lax.ppermute(sent, "xh", SWAP)
    key_weight_grad, value_weight_grad = last_sum(kept, got, [stream_grad])
    return texts[0], texts[1], key_weight_grad, value_weight_grad, stream_grad


def solution(mesh):
    fine = Mesh(mesh.devices.reshape(4, 2, 4, 2, 2), ("z", "xh", "y", "xl", "c"))
    dp, mp = ("z", "xh", "y"), ("xl", "c")
    placed = (
        P(mp, dp, None),
        P(dp + mp, None),
        P(),
        P(None, mp),
        P(None, mp),
        P(dp, None, mp),
        P(dp, None, mp),
        P(dp),
        P(dp, None),
    )
    return jax.shard_map(
        local,
        mesh=fine,
        in_specs=placed,
        out_specs=(P(dp, None, mp), P(dp, None, mp), P(dp, mp), P(dp, mp), P(dp + mp, None)),
        check_vma=False,
    )
```

```python
import functools

import jax
import jax.numpy as jnp
from jax import lax
from jax.experimental import pallas as pl
from jax.experimental.pallas import tpu as pltpu
from jax.sharding import Mesh, PartitionSpec as P

HD = 256
RING = 4
BF = jnp.bfloat16
F32 = jnp.float32
SWAP = [(0, 1), (1, 0)]
MIB = 1024 * 1024
LANES = 512
CUTS = 4
ANYWHERE = pl.BlockSpec(memory_space=pl.ANY)


def dot(left, right, dims=((1,), (0,))):
    return lax.dot_general(left, right, (dims, ((), ())), preferred_element_type=F32)


def shape(dims, kind=BF):
    return jax.ShapeDtypeStruct(dims, kind)


def cost(flops, moved, special=0):
    return pl.CostEstimate(flops=flops, bytes_accessed=moved, transcendentals=special)


def call(body, grid, scalars, ins, in_specs, outs, out_specs, scratch=(), after=(), mib=20, **more):
    count, waits = len(scalars) + len(ins), len(after)

    def with_waits(*refs):
        body(*refs[:count], *refs[count + waits :])

    return pl.pallas_call(
        with_waits,
        grid_spec=pltpu.PrefetchScalarGridSpec(
            num_scalar_prefetch=len(scalars),
            grid=grid,
            in_specs=list(in_specs) + [ANYWHERE] * waits,
            out_specs=out_specs,
            scratch_shapes=scratch,
        ),
        out_shape=outs,
        compiler_params=pltpu.CompilerParams(vmem_limit_bytes=mib * MIB),
        **more,
    )(*scalars, *ins, *after)


def part_of_body(image, where_ref, part_in, share_in, out, hold, load_sems, store_sems):
    rows = out.shape[0]
    step = rows // 4
    start = (image * 2 + 1 - where_ref[0]) * rows

    def load(n):
        source = part_in.at[0, pl.ds(pl.multiple_of(start + n * step, step), step)]
        return pltpu.make_async_copy(source, hold.at[pl.ds(n * step, step)], load_sems.at[n])

    def store(n):
        at = pl.ds(n * step, step)
        return pltpu.make_async_copy(hold.at[at], out.at[at], store_sems.at[n])

    for n in range(4):
        load(n).start()
    for n in range(4):
        load(n).wait()
        store(n).start()
    for n in range(4):
        store(n).wait()


def part_of(image, where, vit_partial, vit_residual, after):
    return call(
        functools.partial(part_of_body, image),
        (1,),
        [where],
        [vit_partial, vit_residual],
        [ANYWHERE] * 2,
        shape(vit_residual.shape),
        ANYWHERE,
        scratch=[
            pltpu.VMEM(vit_residual.shape, BF),
            pltpu.SemaphoreType.DMA((4,)),
            pltpu.SemaphoreType.DMA((4,)),
        ],
        after=after,
        mib=60,
    )


def lanes(width):
    return [slice(start, start + LANES) for start in range(0, width, LANES)]


def chip_sum_body(image, where_ref, part_ref, theirs_ref, residual_ref, out_ref):
    scale = jnp.where(where_ref[1] == image, 1.0, 0.0)
    for at in lanes(out_ref.shape[1]):
        total = part_ref[0, :, at].astype(F32) + theirs_ref[:, at].astype(F32)
        out_ref[:, at] = (total + scale * residual_ref[:, at].astype(F32)).astype(BF)


def chip_sum(image, where, vit_partial, theirs, residual):
    rows, width = residual.shape
    step = rows // 4
    plain = pl.BlockSpec((step, width), lambda i, where_ref: (i, 0))
    return call(
        functools.partial(chip_sum_body, image),
        (4,),
        [where],
        [vit_partial, theirs, residual],
        [
            pl.BlockSpec(
                (1, step, width), lambda i, where_ref: (0, (image * 2 + where_ref[0]) * 4 + i, 0)
            ),
            plain,
            plain,
        ],
        shape((rows, width)),
        plain,
        cost_estimate=cost(0, 8 * rows * width),
    )


def centre_rows(first_ref, second_ref, hold_ref, rows):
    width = hold_ref.shape[1]
    total = 0.0
    for at in lanes(width):
        stream = first_ref[rows, at].astype(F32) + second_ref[rows, at].astype(F32)
        hold_ref[rows, at] = stream
        total = total + stream
    row_mean = jnp.sum(total, axis=-1, keepdims=True) * (1.0 / width)
    total = 0.0
    for at in lanes(width):
        centred = hold_ref[rows, at] - row_mean
        hold_ref[rows, at] = centred
        total = total + centred * centred
    return lax.rsqrt(jnp.sum(total, axis=-1, keepdims=True) * (1.0 / width) + 1e-06)


def norm_body(mine_ref, other_ref, gain_ref, out_ref, hold_ref):
    rows = slice(None)
    inv_std = centre_rows(mine_ref, other_ref, hold_ref, rows)
    for at in lanes(out_ref.shape[1]):
        out_ref[:, at] = (hold_ref[:, at] * inv_std * gain_ref[:, at]).astype(BF)


def norm(mine, other, gain, after):
    rows, width = mine.shape
    plain = pl.BlockSpec((rows // 4, width), lambda i: (i, 0))
    return call(
        norm_body,
        (4,),
        [],
        [mine, other, gain],
        [plain, plain, pl.BlockSpec((1, width), lambda i: (0, 0))],
        shape((rows, width)),
        plain,
        scratch=[pltpu.VMEM((rows // 4, width), F32)],
        after=after,
        cost_estimate=cost(0, 6 * rows * width),
    )


def norm_back_body(where_ref, gain_ref, *refs):
    first, second = refs[:4], refs[4:8]
    out, held, hold, result, load_sems, store_sems = refs[8:]
    width = hold.shape[1]
    rows = held.shape[1] // 4

    def loads(n, group):
        at = pl.ds(n * rows, rows)
        return [
            pltpu.make_async_copy(source.at[at], held.at[j, at], load_sems.at[j, n])
            for j, source in enumerate(group)
        ]

    for side, group in enumerate((first, second)):

        @pl.when(where_ref[1] == side)
        def _(group=group):
            for n in range(4):
                for copy in loads(n, group):
                    copy.start()

    stores = []
    for n in range(4):
        for copy in loads(n, first):
            copy.wait()
        part = slice(n * rows, (n + 1) * rows)
        inv_std = centre_rows(held.at[0], held.at[1], hold, part)
        sum_grad = sum_proj = 0.0
        for at in lanes(width):
            scaled = held[2, part, at].astype(F32) + held[3, part, at].astype(F32)
            scaled = scaled * gain_ref[:, at]
            result[part, at] = scaled
            sum_grad = sum_grad + scaled
            sum_proj = sum_proj + scaled * hold[part, at]
        mean_grad = jnp.sum(sum_grad, axis=-1, keepdims=True) * (1.0 / width)
        mean_proj = jnp.sum(sum_proj, axis=-1, keepdims=True) * inv_std * (1.0 / width)
        for at in lanes(width):
            normal_rows = hold[part, at] * inv_std
            result[part, at] = inv_std * (result[part, at] - mean_grad - normal_rows * mean_proj)
        at = pl.ds(n * rows, rows)
        stores.append(pltpu.make_async_copy(result.at[at], out.at[at], store_sems.at[n]))
        stores[n].start()
    for copy in stores:
        copy.wait()


def norm_back(where, gain, first, second):
    rows, width = first[0].shape
    return call(
        norm_back_body,
        (1,),
        [where],
        [gain, *first, *second],
        [pl.BlockSpec((1, width), lambda i, where_ref: (0, 0))] + [ANYWHERE] * 8,
        shape((rows, width), F32),
        ANYWHERE,
        scratch=[
            pltpu.VMEM((4, rows, width), BF),
            pltpu.VMEM((rows, width), F32),
            pltpu.VMEM((rows, width), F32),
            pltpu.SemaphoreType.DMA((4, 4)),
            pltpu.SemaphoreType.DMA((4,)),
        ],
        mib=56,
        cost_estimate=cost(0, 12 * rows * width),
    )


def ring_sum_body(where_ref, *refs):
    *blocks, kept_ref, sent_ref = refs
    rows = kept_ref.shape[0]

    def total(block):
        at = pl.ds(pl.multiple_of(block * rows, rows), rows)
        return sum(ref[at].astype(F32) for ref in blocks)

    sent_ref[...] = total(1 - where_ref[4]).astype(BF)
    kept_ref[...] = total(where_ref[4])


def ring_sum(where, blocks, after):
    rows, width = blocks[0].shape
    whole = pl.BlockSpec((rows, width), lambda i, where_ref: (0, 0))
    half = pl.BlockSpec((rows // 2, width), lambda i, where_ref: (0, 0))
    return call(
        ring_sum_body,
        (1,),
        [where],
        blocks,
        [whole] * len(blocks),
        [shape((rows // 2, width), F32), shape((rows // 2, width))],
        [half, half],
        after=after,
        cost_estimate=cost(0, 12 * rows * width),
    )


def last_sum_body(kept_ref, got_ref, key_ref, value_ref):
    total = kept_ref[...] + got_ref[...].astype(F32)
    width = key_ref.shape[1]
    key_ref[...] = total[:, :width]
    value_ref[...] = total[:, width:]


def last_sum(kept, got, after):
    rows, width = kept.shape
    whole = pl.BlockSpec((rows, width), lambda i: (0, 0))
    half = pl.BlockSpec((rows, width // 2), lambda i: (0, 0))
    return call(
        last_sum_body,
        (1,),
        [],
        [kept, got],
        [whole, whole],
        [shape((rows, width // 2), F32)] * 2,
        [half, half],
        after=after,
        mib=60,
        cost_estimate=cost(0, 10 * rows * width),
    )


def strips_body(where_ref, own_in, far_in, *rest):
    outs = rest[:RING]
    own_ref, far_ref, hold, load_sems, store_sems = rest[RING:]
    total_rows, width = own_ref.shape
    step = total_rows // 4
    piece = width // (2 * RING * RING)
    refs = (own_ref, far_ref)

    def load(n, half):
        at = pl.ds(n * step, step)
        source = (own_in, far_in)[half]
        return pltpu.make_async_copy(source.at[at], refs[half].at[at], load_sems.at[half, n])

    def store(n, k):
        at = pl.ds(n * step, step)
        source = hold.at[lax.rem(where_ref[2] + k, RING)]
        return pltpu.make_async_copy(source.at[:, at], outs[k].at[:, at], store_sems.at[k, n])

    def fill(n, along_y):
        at = slice(n * step, (n + 1) * step)
        for half in range(2):
            for a in range(RING):
                for b in range(RING):
                    for x in range(2):
                        z, y = (b, a) if along_y else (a, b)
                        start = ((z * 2 + x) * RING + y) * piece
                        spot = (b * 2 + x) * piece
                        hold[a, half, at, spot : spot + piece] = refs[half][at, start : start + piece]

    for n in range(4):
        for half in range(2):
            load(n, half).start()
    for n in range(4):
        for half in range(2):
            load(n, half).wait()
        pl.when(where_ref[0] == 0)(functools.partial(fill, n, True))
        pl.when(where_ref[0] == 1)(functools.partial(fill, n, False))
        for k in range(RING):
            store(n, k).start()
    for n in range(4):
        for k in range(RING):
            store(n, k).wait()


def strips(where, own, far, after):
    rows, width = own.shape
    part = width // RING
    return call(
        strips_body,
        (1,),
        [where],
        [own, far],
        [ANYWHERE] * 2,
        [shape((2, rows, part))] * RING,
        [ANYWHERE] * RING,
        scratch=[
            pltpu.VMEM((rows, width), BF),
            pltpu.VMEM((rows, width), BF),
            pltpu.VMEM((RING, 2, rows, part), BF),
            pltpu.SemaphoreType.DMA((2, 4)),
            pltpu.SemaphoreType.DMA((RING, 4)),
        ],
        after=after,
        cost_estimate=cost(0, 8 * rows * width),
    )


def image_body(image, pick_ref, len_ref, own_in, far_in, key_in, value_in, q_in, g_in, *rest):
    context_out, query_grad_out, near_out, away_out, grads_ref = rest[-19:-14]
    rows, keys, values, total, q_ref, g_ref, context_ref, query_grad_ref, back = rest[-14:-5]
    row_sems, weight_sems, text_sems, back_sems, done_sems = rest[-5:]
    half = rows.shape[0] // 2
    chunk = keys.shape[0] // CUTS
    width = keys.shape[1]
    example = pick_ref[image]
    limit = len_ref[example]

    def at(n):
        return pl.ds(pl.multiple_of(n * chunk, chunk), chunk)

    def row_loads(n):
        return [
            pltpu.make_async_copy(own_in.at[:, at(n)], rows.at[:half, at(n)], row_sems.at[0, n]),
            pltpu.make_async_copy(far_in.at[:, at(n)], rows.at[half:, at(n)], row_sems.at[1, n]),
        ]

    def weight_loads(n):
        return [
            pltpu.make_async_copy(key_in.at[at(n)], keys.at[at(n)], weight_sems.at[0, n]),
            pltpu.make_async_copy(value_in.at[at(n)], values.at[at(n)], weight_sems.at[1, n]),
        ]

    def back_stores(n):
        return [
            pltpu.make_async_copy(back.at[:half, at(n)], near_out.at[:, at(n)], back_sems.at[0, n]),
            pltpu.make_async_copy(back.at[half:, at(n)], away_out.at[:, at(n)], back_sems.at[1, n]),
        ]

    text_loads = [
        pltpu.make_async_copy(q_in.at[example], q_ref, text_sems.at[0]),
        pltpu.make_async_copy(g_in.at[example], g_ref, text_sems.at[1]),
    ]
    text_stores = [
        pltpu.make_async_copy(context_ref, context_out.at[example], done_sems.at[0]),
        pltpu.make_async_copy(query_grad_ref, query_grad_out.at[example], done_sems.at[1]),
    ]

    @pl.loop(0, CUTS)
    def _(n):
        for copy in row_loads(n) + weight_loads(n):
            copy.start()

    for copy in text_loads:
        copy.start()
    total[...] = jnp.zeros_like(total)

    @pl.loop(0, CUTS)
    def _(n):
        for copy in row_loads(n) + weight_loads(n):
            copy.wait()
        left = rows[:, at(n)]
        total[:, :width] += dot(left, keys[at(n)])
        total[:, width:] += dot(left, values[at(n)])

    for copy in text_loads:
        copy.wait()
    mask = lax.broadcasted_iota(jnp.int32, (q_ref.shape[0], 1), 0) < limit
    for head in range(width // HD):
        key_at = slice(head * HD, (head + 1) * HD)
        value_at = slice(width + head * HD, width + (head + 1) * HD)
        key, value = total[:, key_at].astype(BF), total[:, value_at].astype(BF)
        q = q_ref[:, key_at]
        scores = dot(q, key, ((1,), (1,))) * HD ** (-0.5)
        exp_terms = jnp.exp(scores - jnp.max(scores, axis=-1, keepdims=True))
        softmax_w = exp_terms / jnp.sum(exp_terms, axis=-1, keepdims=True)
        weights_bf = softmax_w.astype(BF)
        context_ref[:, key_at] = jnp.where(mask, dot(weights_bf, value), 0.0)
        upstream = jnp.where(mask, g_ref[:, key_at].astype(F32), 0.0).astype(BF)
        weight_grad = dot(upstream, value, ((1,), (1,)))
        centre = jnp.sum(weight_grad * softmax_w, axis=-1, keepdims=True)
        score_grad = (softmax_w * (weight_grad - centre) * HD ** (-0.5)).astype(BF)
        query_grad_ref[:, key_at] = dot(score_grad, key)
        grads_ref[:, key_at] = dot(score_grad, q, ((0,), (0,))).astype(BF)
        grads_ref[:, value_at] = dot(weights_bf, upstream, ((0,), (0,))).astype(BF)
    for copy in text_stores:
        copy.start()

    @pl.loop(0, CUTS)
    def _(n):
        term = dot(grads_ref[:, :width], keys[at(n)], ((1,), (1,)))
        term = term + dot(grads_ref[:, width:], values[at(n)], ((1,), (1,)))
        back[:, at(n)] = term.astype(BF)
        for copy in back_stores(n):
            copy.start()

    @pl.loop(0, CUTS)
    def _(n):
        for copy in back_stores(n):
            copy.wait()

    for copy in text_stores:
        copy.wait()


def image_step(
    image, pick, text_len, own, far, key_weight, value_weight, queries, context_grad, partly, after
):
    text_rows, width = queries.shape[1:]
    half, depth = own.shape
    flat = (2 * half, 2 * width)
    sems = pltpu.SemaphoreType.DMA
    return call(
        functools.partial(image_body, image),
        (1,),
        [pick, text_len],
        [own, far, key_weight, value_weight, queries, context_grad, *partly],
        [ANYWHERE] * (6 + len(partly)),
        [shape(queries.shape, F32)] * 2 + [shape(own.shape)] * 2 + [shape(flat)],
        [ANYWHERE] * 4 + [pl.BlockSpec(flat, lambda i, *scalars: (0, 0))],
        scratch=[
            pltpu.VMEM((2 * half, depth), BF),
            pltpu.VMEM(key_weight.shape, BF),
            pltpu.VMEM(key_weight.shape, BF),
            pltpu.VMEM(flat, F32),
            pltpu.VMEM((text_rows, width), BF),
            pltpu.VMEM((text_rows, width), BF),
            pltpu.VMEM((text_rows, width), F32),
            pltpu.VMEM((text_rows, width), F32),
            pltpu.VMEM((2 * half, depth), BF),
            sems((2, CUTS)),
            sems((2, CUTS)),
            sems((2,)),
            sems((2, CUTS)),
            sems((2,)),
        ],
        after=after,
        input_output_aliases={8: 0, 9: 1} if partly else {},
        mib=44,
        cost_estimate=cost(
            16 * half * depth * width + 24 * text_rows * half * width,
            4 * depth * (2 * half + width) + 12 * text_rows * width,
            2 * text_rows * half * width // HD,
        ),
    )


def weight_grad_body(first, pieces, where_ref, *refs):
    lefts_in, rights_in, rest = refs[:RING], refs[RING : RING + pieces], refs[RING + pieces :]
    left, right, result, left_sems, right_sems, store_sems = rest[-6:]
    outs = rest[:1] if first else rest[1:-6]
    rows = right.shape[0] // RING
    chunk, width = result.shape[1:]
    half = rows // 2
    wide = width // 2

    def right_loads():
        start = 0
        for k, source in enumerate(rights_in):
            target = right.at[pl.ds(start, source.shape[0])]
            start += source.shape[0]
            yield pltpu.make_async_copy(source, target, right_sems.at[k])

    def left_load(n, k, h):
        columns = pl.ds(pl.multiple_of(lax.rem(where_ref[3] + n, RING) * chunk, chunk), chunk)
        at = pl.ds(k * rows + h * half, half)
        source = lefts_in[k].at[h, :, columns]
        return pltpu.make_async_copy(source, left.at[n, at], left_sems.at[n, k, h])

    def stores(n):
        if first:
            return [pltpu.make_async_copy(result.at[n], outs[0].at[n], store_sems.at[n])]
        if n != 2:
            target = outs[(0, 1, None, 4)[n]]
            return [pltpu.make_async_copy(result.at[n], target, store_sems.at[n])]
        cut = chunk // 2
        top, bottom = pl.ds(0, cut), pl.ds(cut, cut)
        return [
            pltpu.make_async_copy(result.at[n, top], outs[2], store_sems.at[n]),
            pltpu.make_async_copy(result.at[n, bottom], outs[3], store_sems.at[RING]),
        ]

    each = [(k, h) for k in range(RING) for h in range(2)]
    order = (2, 1, 3, 0)
    for copy in right_loads():
        copy.start()
    for n in order:
        for k, h in each:
            left_load(n, k, h).start()
    for copy in right_loads():
        copy.wait()
    for n in order:
        for k, h in each:
            left_load(n, k, h).wait()
        for columns in (slice(0, wide), slice(wide, width)):
            total = dot(left[n], right[:, columns], ((0,), (0,)))
            if not first:
                total = total + rest[0][n, :, columns].astype(F32)
            result[n, :, columns] = total.astype(BF)
        for copy in stores(n):
            copy.start()
    for n in order:
        for copy in stores(n):
            copy.wait()


def weight_grad(where, lefts, rights, so_far=None, after=()):
    halves, rows, part = lefts[0].shape
    width = rights[0].shape[1]
    chunk, pieces = part // RING, len(rights)
    first = so_far is None
    whole = (RING, chunk, width)
    heights = [chunk, chunk, chunk // 2, chunk // 2, chunk]
    outs = [shape(whole)] if first else [shape((height, width)) for height in heights]
    return call(
        functools.partial(weight_grad_body, first, pieces),
        (1,),
        [where],
        [*lefts, *rights] + ([] if first else [so_far]),
        [ANYWHERE] * (RING + pieces)
        + ([] if first else [pl.BlockSpec(whole, lambda i, where_ref: (0, 0, 0))]),
        outs,
        [ANYWHERE] * len(outs),
        scratch=[
            pltpu.VMEM((RING, RING * halves * rows, chunk), BF),
            pltpu.VMEM((RING * halves * rows, width), BF),
            pltpu.VMEM(whole, BF),
            pltpu.SemaphoreType.DMA((RING, RING, 2)),
            pltpu.SemaphoreType.DMA((pieces,)),
            pltpu.SemaphoreType.DMA((RING + 1,)),
        ],
        after=after,
        cost_estimate=cost(0, 0),
    )


def relay_body(up_ref, got_up_ref, down_ref, got_down_ref, up_out, down_out):
    cut = got_up_ref.shape[0]
    up_out[:cut] = (up_ref[:cut].astype(F32) + got_up_ref[...].astype(F32)).astype(BF)
    up_out[cut:] = up_ref[cut:]
    down_out[:cut] = down_ref[:cut]
    down_out[cut:] = (down_ref[cut:].astype(F32) + got_down_ref[...].astype(F32)).astype(BF)


def relay(up, got_up, down, got_down):
    whole = pl.BlockSpec(up.shape, lambda i: (0, 0))
    half = pl.BlockSpec(got_up.shape, lambda i: (0, 0))
    return call(
        relay_body,
        (1,),
        [],
        [up, got_up, down, got_down],
        [whole, half, whole, half],
        [shape(up.shape)] * 2,
        [whole, whole],
        cost_estimate=cost(0, 0),
    )


def later(array, after):
    return call(
        lambda *refs: None,
        (1,),
        [],
        [array],
        [ANYWHERE],
        shape(array.shape, array.dtype),
        ANYWHERE,
        after=after,
        input_output_aliases={0: 0},
    )


def hop(first, distance):
    pairs = []
    for z in range(RING):
        for y in range(RING):
            for core in range(2):
                along_y = (core == 0) == first
                to = (z, (y + distance) % RING) if along_y else ((z + distance) % RING, y)
                pairs.append(((z * RING + y) * 2 + core, (to[0] * RING + to[1]) * 2 + core))
    return pairs


def rotate(array, first, distance):
    return lax.ppermute(array, ("z", "y", "c"), hop(first, distance))


def local(
    vit_partial,
    vit_residual,
    ln_gain,
    key_weight,
    value_weight,
    queries,
    context_grad,
    text_len,
    image_pick,
):
    share, model_width = vit_residual.shape
    width = key_weight.shape[1]
    core, side, cross = lax.axis_index("c"), lax.axis_index("xl"), lax.axis_index("xh")
    y, z = lax.axis_index("y"), lax.axis_index("z")
    where = jnp.stack([core, side, jnp.where(core == 0, y, z), jnp.where(core == 0, z, y), cross])
    pick = image_pick[0]
    gain = ln_gain[None, :]

    mine, other, after = [], [], []
    for image in range(2):
        sent = part_of(image, where, vit_partial, vit_residual, after)
        after = [sent]
        theirs = lax.ppermute(sent, "c", SWAP)
        mine.append(chip_sum(image, where, vit_partial, theirs, vit_residual))
        other.append(lax.ppermute(mine[image], "xl", SWAP))

    def spread(array, firsts):
        return [array] + [rotate(firsts[k], True, k) for k in range(1, RING)]

    def core_sum(near_rows, away_rows):
        theirs = lax.ppermute(away_rows, "c", SWAP)
        return (near_rows.astype(F32) + theirs.astype(F32)).astype(BF)

    def step(image, own, far, texts, after):
        given = (key_weight, value_weight, queries, context_grad)
        return image_step(image, pick, text_len, own, far, *given, texts, after)

    own = norm(mine[0], other[0], gain, [mine[1]])
    far = lax.ppermute(own, "c", SWAP)
    pieces = strips(where, own, far, [])
    lefts = spread(pieces[0], pieces)
    *texts, near_rows, away_rows, grads = step(0, own, far, [], [pieces[0]])
    grads = later(grads, [lefts[1], lefts[3]])
    rights = spread(grads, [grads] * RING)

    own = norm(mine[1], other[1], gain, [near_rows, lefts[2], *rights[1:]])
    far = lax.ppermute(own, "c", SWAP)
    pieces = strips(where, own, far, [])
    last_lefts = spread(pieces[0], pieces)
    near_0, away_0 = near_rows, away_rows
    *texts, near_rows, away_rows, grads = step(1, own, far, texts, [pieces[0]])
    share_0 = core_sum(near_0, later(away_0, [pieces[0]]))
    grads = later(grads, last_lefts[1:])
    last_rights = spread(grads, [grads] * RING)
    (so_far,) = weight_grad(where, lefts, rights, after=[grads, share_0])
    share_1 = core_sum(near_rows, later(away_rows, [grads]))

    from_second = lax.ppermute(share_0, "xl", [(1, 0)])
    from_first = lax.ppermute(share_1, "xl", [(0, 1)])
    blocks = weight_grad(where, last_lefts, last_rights, so_far, [share_0, share_1])
    kept, up, across_up, across_down, down = blocks
    got_up = rotate(across_up, False, 1)
    got_down = rotate(across_down, False, RING - 1)
    up, down = relay(up, got_up, down, got_down)
    got = [rotate(up, False, 1), rotate(down, False, RING - 1)]
    stream_grad = norm_back(
        where,
        gain,
        [mine[0], other[0], share_0, from_second],
        [mine[1], other[1], share_1, from_first],
    )
    kept, sent = ring_sum(where, [kept, *got], [from_first, from_second])
    got = lax.ppermute(sent, "xh", SWAP)
    key_weight_grad, value_weight_grad = last_sum(kept, got, [stream_grad])
    return texts[0], texts[1], key_weight_grad, value_weight_grad, stream_grad


def solution(mesh):
    fine = Mesh(mesh.devices.reshape(4, 2, 4, 2, 2), ("z", "xh", "y", "xl", "c"))
    dp, mp = ("z", "xh", "y"), ("xl", "c")
    placed = (
        P(mp, dp, None),
        P(dp + mp, None),
        P(),
        P(None, mp),
        P(None, mp),
        P(dp, None, mp),
        P(dp, None, mp),
        P(dp),
        P(dp, None),
    )
    return jax.shard_map(
        local,
        mesh=fine,
        in_specs=placed,
        out_specs=(P(dp, None, mp), P(dp, None, mp), P(dp, mp), P(dp, mp), P(dp + mp, None)),
        check_vma=False,
    )
```

```python
import functools

import jax
import jax.numpy as jnp
from jax import lax
from jax.experimental import pallas as pl
from jax.experimental.pallas import tpu as pltpu
from jax.sharding import Mesh, PartitionSpec as P

HD = 256
RING = 4
BF = jnp.bfloat16
F32 = jnp.float32
SWAP = [(0, 1), (1, 0)]
MIB = 1024 * 1024
LANES = 512
CUTS = 4
ANYWHERE = pl.BlockSpec(memory_space=pl.ANY)


def dot(left, right, dims=((1,), (0,))):
    return lax.dot_general(left, right, (dims, ((), ())), preferred_element_type=F32)


def shape(dims, kind=BF):
    return jax.ShapeDtypeStruct(dims, kind)


def cost(flops, moved, special=0):
    return pl.CostEstimate(flops=flops, bytes_accessed=moved, transcendentals=special)


def call(body, grid, scalars, ins, in_specs, outs, out_specs, scratch=(), after=(), mib=20, **more):
    count, waits = len(scalars) + len(ins), len(after)

    def with_waits(*refs):
        body(*refs[:count], *refs[count + waits :])

    return pl.pallas_call(
        with_waits,
        grid_spec=pltpu.PrefetchScalarGridSpec(
            num_scalar_prefetch=len(scalars),
            grid=grid,
            in_specs=list(in_specs) + [ANYWHERE] * waits,
            out_specs=out_specs,
            scratch_shapes=scratch,
        ),
        out_shape=outs,
        compiler_params=pltpu.CompilerParams(vmem_limit_bytes=mib * MIB),
        **more,
    )(*scalars, *ins, *after)


def part_of_body(image, where_ref, part_in, share_in, out, hold, load_sems, store_sems):
    rows = out.shape[0]
    step = rows // 4
    start = (image * 2 + 1 - where_ref[0]) * rows

    def load(n):
        source = part_in.at[0, pl.ds(pl.multiple_of(start + n * step, step), step)]
        return pltpu.make_async_copy(source, hold.at[pl.ds(n * step, step)], load_sems.at[n])

    def store(n):
        at = pl.ds(n * step, step)
        return pltpu.make_async_copy(hold.at[at], out.at[at], store_sems.at[n])

    for n in range(4):
        load(n).start()
    for n in range(4):
        load(n).wait()
        store(n).start()
    for n in range(4):
        store(n).wait()


def part_of(image, where, vit_partial, vit_residual, after):
    return call(
        functools.partial(part_of_body, image),
        (1,),
        [where],
        [vit_partial, vit_residual],
        [ANYWHERE] * 2,
        shape(vit_residual.shape),
        ANYWHERE,
        scratch=[
            pltpu.VMEM(vit_residual.shape, BF),
            pltpu.SemaphoreType.DMA((4,)),
            pltpu.SemaphoreType.DMA((4,)),
        ],
        after=after,
        mib=60,
    )


def lanes(width):
    return [slice(start, start + LANES) for start in range(0, width, LANES)]


def chip_sum_body(image, where_ref, part_ref, theirs_ref, residual_ref, out_ref):
    scale = jnp.where(where_ref[1] == image, 1.0, 0.0)
    for at in lanes(out_ref.shape[1]):
        total = part_ref[0, :, at].astype(F32) + theirs_ref[:, at].astype(F32)
        out_ref[:, at] = (total + scale * residual_ref[:, at].astype(F32)).astype(BF)


def chip_sum(image, where, vit_partial, theirs, residual):
    rows, width = residual.shape
    step = rows // 4
    plain = pl.BlockSpec((step, width), lambda i, where_ref: (i, 0))
    return call(
        functools.partial(chip_sum_body, image),
        (4,),
        [where],
        [vit_partial, theirs, residual],
        [
            pl.BlockSpec(
                (1, step, width), lambda i, where_ref: (0, (image * 2 + where_ref[0]) * 4 + i, 0)
            ),
            plain,
            plain,
        ],
        shape((rows, width)),
        plain,
        cost_estimate=cost(0, 8 * rows * width),
    )


def centre_rows(first_ref, second_ref, hold_ref, rows):
    width = hold_ref.shape[1]
    total = 0.0
    for at in lanes(width):
        stream = first_ref[rows, at].astype(F32) + second_ref[rows, at].astype(F32)
        hold_ref[rows, at] = stream
        total = total + stream
    row_mean = jnp.sum(total, axis=-1, keepdims=True) * (1.0 / width)
    total = 0.0
    for at in lanes(width):
        centred = hold_ref[rows, at] - row_mean
        hold_ref[rows, at] = centred
        total = total + centred * centred
    return lax.rsqrt(jnp.sum(total, axis=-1, keepdims=True) * (1.0 / width) + 1e-06)


def norm_body(mine_ref, other_ref, gain_ref, out_ref, hold_ref):
    rows = slice(None)
    inv_std = centre_rows(mine_ref, other_ref, hold_ref, rows)
    for at in lanes(out_ref.shape[1]):
        out_ref[:, at] = (hold_ref[:, at] * inv_std * gain_ref[:, at]).astype(BF)


def norm(mine, other, gain, after):
    rows, width = mine.shape
    plain = pl.BlockSpec((rows // 4, width), lambda i: (i, 0))
    return call(
        norm_body,
        (4,),
        [],
        [mine, other, gain],
        [plain, plain, pl.BlockSpec((1, width), lambda i: (0, 0))],
        shape((rows, width)),
        plain,
        scratch=[pltpu.VMEM((rows // 4, width), F32)],
        after=after,
        cost_estimate=cost(0, 6 * rows * width),
    )


def norm_back_body(where_ref, gain_ref, *refs):
    first, second = refs[:4], refs[4:8]
    out, held, hold, result, load_sems, store_sems = refs[8:]
    width = hold.shape[1]
    rows = held.shape[1] // 4

    def loads(n, group):
        at = pl.ds(n * rows, rows)
        return [
            pltpu.make_async_copy(source.at[at], held.at[j, at], load_sems.at[j, n])
            for j, source in enumerate(group)
        ]

    for side, group in enumerate((first, second)):

        @pl.when(where_ref[1] == side)
        def _(group=group):
            for n in range(4):
                for copy in loads(n, group):
                    copy.start()

    stores = []
    for n in range(4):
        for copy in loads(n, first):
            copy.wait()
        part = slice(n * rows, (n + 1) * rows)
        inv_std = centre_rows(held.at[0], held.at[1], hold, part)
        sum_grad = sum_proj = 0.0
        for at in lanes(width):
            scaled = held[2, part, at].astype(F32) + held[3, part, at].astype(F32)
            scaled = scaled * gain_ref[:, at]
            result[part, at] = scaled
            sum_grad = sum_grad + scaled
            sum_proj = sum_proj + scaled * hold[part, at]
        mean_grad = jnp.sum(sum_grad, axis=-1, keepdims=True) * (1.0 / width)
        mean_proj = jnp.sum(sum_proj, axis=-1, keepdims=True) * inv_std * (1.0 / width)
        for at in lanes(width):
            normal_rows = hold[part, at] * inv_std
            result[part, at] = inv_std * (result[part, at] - mean_grad - normal_rows * mean_proj)
        at = pl.ds(n * rows, rows)
        stores.append(pltpu.make_async_copy(result.at[at], out.at[at], store_sems.at[n]))
        stores[n].start()
    for copy in stores:
        copy.wait()


def norm_back(where, gain, first, second):
    rows, width = first[0].shape
    return call(
        norm_back_body,
        (1,),
        [where],
        [gain, *first, *second],
        [pl.BlockSpec((1, width), lambda i, where_ref: (0, 0))] + [ANYWHERE] * 8,
        shape((rows, width), F32),
        ANYWHERE,
        scratch=[
            pltpu.VMEM((4, rows, width), BF),
            pltpu.VMEM((rows, width), F32),
            pltpu.VMEM((rows, width), F32),
            pltpu.SemaphoreType.DMA((4, 4)),
            pltpu.SemaphoreType.DMA((4,)),
        ],
        mib=56,
        cost_estimate=cost(0, 12 * rows * width),
    )


def ring_sum_body(where_ref, *refs):
    *blocks, kept_ref, sent_ref = refs
    rows = kept_ref.shape[0]

    def total(block):
        at = pl.ds(pl.multiple_of(block * rows, rows), rows)
        return sum(ref[at].astype(F32) for ref in blocks)

    sent_ref[...] = total(1 - where_ref[4]).astype(BF)
    kept_ref[...] = total(where_ref[4])


def ring_sum(where, blocks, after):
    rows, width = blocks[0].shape
    whole = pl.BlockSpec((rows, width), lambda i, where_ref: (0, 0))
    half = pl.BlockSpec((rows // 2, width), lambda i, where_ref: (0, 0))
    return call(
        ring_sum_body,
        (1,),
        [where],
        blocks,
        [whole] * len(blocks),
        [shape((rows // 2, width), F32), shape((rows // 2, width))],
        [half, half],
        after=after,
        cost_estimate=cost(0, 12 * rows * width),
    )


def last_sum_body(kept_ref, got_ref, key_ref, value_ref):
    total = kept_ref[...] + got_ref[...].astype(F32)
    width = key_ref.shape[1]
    key_ref[...] = total[:, :width]
    value_ref[...] = total[:, width:]


def last_sum(kept, got, after):
    rows, width = kept.shape
    whole = pl.BlockSpec((rows, width), lambda i: (0, 0))
    half = pl.BlockSpec((rows, width // 2), lambda i: (0, 0))
    return call(
        last_sum_body,
        (1,),
        [],
        [kept, got],
        [whole, whole],
        [shape((rows, width // 2), F32)] * 2,
        [half, half],
        after=after,
        mib=60,
        cost_estimate=cost(0, 10 * rows * width),
    )


def strips_body(where_ref, own_in, far_in, *rest):
    outs = rest[:RING]
    own_ref, far_ref, hold, load_sems, store_sems = rest[RING:]
    total_rows, width = own_ref.shape
    step = total_rows // 4
    piece = width // (2 * RING * RING)
    refs = (own_ref, far_ref)

    def load(n, half):
        at = pl.ds(n * step, step)
        source = (own_in, far_in)[half]
        return pltpu.make_async_copy(source.at[at], refs[half].at[at], load_sems.at[half, n])

    def store(n, k):
        at = pl.ds(n * step, step)
        source = hold.at[lax.rem(where_ref[2] + k, RING)]
        return pltpu.make_async_copy(source.at[:, at], outs[k].at[:, at], store_sems.at[k, n])

    def fill(n, along_y):
        at = slice(n * step, (n + 1) * step)
        for half in range(2):
            for a in range(RING):
                for b in range(RING):
                    for x in range(2):
                        z, y = (b, a) if along_y else (a, b)
                        start = ((z * 2 + x) * RING + y) * piece
                        spot = (b * 2 + x) * piece
                        hold[a, half, at, spot : spot + piece] = refs[half][at, start : start + piece]

    for n in range(4):
        for half in range(2):
            load(n, half).start()
    for n in range(4):
        for half in range(2):
            load(n, half).wait()
        pl.when(where_ref[0] == 0)(functools.partial(fill, n, True))
        pl.when(where_ref[0] == 1)(functools.partial(fill, n, False))
        for k in range(RING):
            store(n, k).start()
    for n in range(4):
        for k in range(RING):
            store(n, k).wait()


def strips(where, own, far, after):
    rows, width = own.shape
    part = width // RING
    return call(
        strips_body,
        (1,),
        [where],
        [own, far],
        [ANYWHERE] * 2,
        [shape((2, rows, part))] * RING,
        [ANYWHERE] * RING,
        scratch=[
            pltpu.VMEM((rows, width), BF),
            pltpu.VMEM((rows, width), BF),
            pltpu.VMEM((RING, 2, rows, part), BF),
            pltpu.SemaphoreType.DMA((2, 4)),
            pltpu.SemaphoreType.DMA((RING, 4)),
        ],
        after=after,
        cost_estimate=cost(0, 8 * rows * width),
    )


def image_body(image, pick_ref, len_ref, own_in, far_in, key_in, value_in, q_in, g_in, *rest):
    context_out, query_grad_out, near_out, away_out, grads_ref = rest[-19:-14]
    rows, keys, values, total, q_ref, g_ref, context_ref, query_grad_ref, back = rest[-14:-5]
    row_sems, weight_sems, text_sems, back_sems, done_sems = rest[-5:]
    half = rows.shape[0] // 2
    chunk = keys.shape[0] // CUTS
    width = keys.shape[1]
    example = pick_ref[image]
    limit = len_ref[example]

    def at(n):
        return pl.ds(pl.multiple_of(n * chunk, chunk), chunk)

    def row_loads(n):
        return [
            pltpu.make_async_copy(own_in.at[:, at(n)], rows.at[:half, at(n)], row_sems.at[0, n]),
            pltpu.make_async_copy(far_in.at[:, at(n)], rows.at[half:, at(n)], row_sems.at[1, n]),
        ]

    def weight_loads(n):
        return [
            pltpu.make_async_copy(key_in.at[at(n)], keys.at[at(n)], weight_sems.at[0, n]),
            pltpu.make_async_copy(value_in.at[at(n)], values.at[at(n)], weight_sems.at[1, n]),
        ]

    def back_stores(n):
        return [
            pltpu.make_async_copy(back.at[:half, at(n)], near_out.at[:, at(n)], back_sems.at[0, n]),
            pltpu.make_async_copy(back.at[half:, at(n)], away_out.at[:, at(n)], back_sems.at[1, n]),
        ]

    text_loads = [
        pltpu.make_async_copy(q_in.at[example], q_ref, text_sems.at[0]),
        pltpu.make_async_copy(g_in.at[example], g_ref, text_sems.at[1]),
    ]
    text_stores = [
        pltpu.make_async_copy(context_ref, context_out.at[example], done_sems.at[0]),
        pltpu.make_async_copy(query_grad_ref, query_grad_out.at[example], done_sems.at[1]),
    ]

    @pl.loop(0, CUTS)
    def _(n):
        for copy in row_loads(n) + weight_loads(n):
            copy.start()

    for copy in text_loads:
        copy.start()
    total[...] = jnp.zeros_like(total)

    @pl.loop(0, CUTS)
    def _(n):
        for copy in row_loads(n) + weight_loads(n):
            copy.wait()
        left = rows[:, at(n)]
        total[:, :width] += dot(left, keys[at(n)])
        total[:, width:] += dot(left, values[at(n)])

    for copy in text_loads:
        copy.wait()
    mask = lax.broadcasted_iota(jnp.int32, (q_ref.shape[0], 1), 0) < limit
    for head in range(width // HD):
        key_at = slice(head * HD, (head + 1) * HD)
        value_at = slice(width + head * HD, width + (head + 1) * HD)
        key, value = total[:, key_at].astype(BF), total[:, value_at].astype(BF)
        q = q_ref[:, key_at]
        scores = dot(q, key, ((1,), (1,))) * HD ** (-0.5)
        exp_terms = jnp.exp(scores - jnp.max(scores, axis=-1, keepdims=True))
        softmax_w = exp_terms / jnp.sum(exp_terms, axis=-1, keepdims=True)
        weights_bf = softmax_w.astype(BF)
        context_ref[:, key_at] = jnp.where(mask, dot(weights_bf, value), 0.0)
        upstream = jnp.where(mask, g_ref[:, key_at].astype(F32), 0.0).astype(BF)
        weight_grad = dot(upstream, value, ((1,), (1,)))
        centre = jnp.sum(weight_grad * softmax_w, axis=-1, keepdims=True)
        score_grad = (softmax_w * (weight_grad - centre) * HD ** (-0.5)).astype(BF)
        query_grad_ref[:, key_at] = dot(score_grad, key)
        grads_ref[:, key_at] = dot(score_grad, q, ((0,), (0,))).astype(BF)
        grads_ref[:, value_at] = dot(weights_bf, upstream, ((0,), (0,))).astype(BF)
    for copy in text_stores:
        copy.start()

    @pl.loop(0, CUTS)
    def _(n):
        term = dot(grads_ref[:, :width], keys[at(n)], ((1,), (1,)))
        term = term + dot(grads_ref[:, width:], values[at(n)], ((1,), (1,)))
        back[:, at(n)] = term.astype(BF)
        for copy in back_stores(n):
            copy.start()

    @pl.loop(0, CUTS)
    def _(n):
        for copy in back_stores(n):
            copy.wait()

    for copy in text_stores:
        copy.wait()


def image_step(
    image, pick, text_len, own, far, key_weight, value_weight, queries, context_grad, partly, after
):
    text_rows, width = queries.shape[1:]
    half, depth = own.shape
    flat = (2 * half, 2 * width)
    sems = pltpu.SemaphoreType.DMA
    return call(
        functools.partial(image_body, image),
        (1,),
        [pick, text_len],
        [own, far, key_weight, value_weight, queries, context_grad, *partly],
        [ANYWHERE] * (6 + len(partly)),
        [shape(queries.shape, F32)] * 2 + [shape(own.shape)] * 2 + [shape(flat)],
        [ANYWHERE] * 4 + [pl.BlockSpec(flat, lambda i, *scalars: (0, 0))],
        scratch=[
            pltpu.VMEM((2 * half, depth), BF),
            pltpu.VMEM(key_weight.shape, BF),
            pltpu.VMEM(key_weight.shape, BF),
            pltpu.VMEM(flat, F32),
            pltpu.VMEM((text_rows, width), BF),
            pltpu.VMEM((text_rows, width), BF),
            pltpu.VMEM((text_rows, width), F32),
            pltpu.VMEM((text_rows, width), F32),
            pltpu.VMEM((2 * half, depth), BF),
            sems((2, CUTS)),
            sems((2, CUTS)),
            sems((2,)),
            sems((2, CUTS)),
            sems((2,)),
        ],
        after=after,
        input_output_aliases={8: 0, 9: 1} if partly else {},
        mib=44,
        cost_estimate=cost(
            16 * half * depth * width + 24 * text_rows * half * width,
            4 * depth * (2 * half + width) + 12 * text_rows * width,
            2 * text_rows * half * width // HD,
        ),
    )


def weight_grad_body(first, pieces, where_ref, *refs):
    lefts_in, rights_in, rest = refs[:RING], refs[RING : RING + pieces], refs[RING + pieces :]
    left, right, result, left_sems, right_sems, store_sems = rest[-6:]
    outs = rest[:1] if first else rest[1:-6]
    rows = right.shape[0] // RING
    chunk, width = result.shape[1:]
    half = rows // 2
    wide = width // 2

    def right_loads():
        start = 0
        for k, source in enumerate(rights_in):
            target = right.at[pl.ds(start, source.shape[0])]
            start += source.shape[0]
            yield pltpu.make_async_copy(source, target, right_sems.at[k])

    def left_load(n, k, h):
        columns = pl.ds(pl.multiple_of(lax.rem(where_ref[3] + n, RING) * chunk, chunk), chunk)
        at = pl.ds(k * rows + h * half, half)
        source = lefts_in[k].at[h, :, columns]
        return pltpu.make_async_copy(source, left.at[n, at], left_sems.at[n, k, h])

    def stores(n):
        if first:
            return [pltpu.make_async_copy(result.at[n], outs[0].at[n], store_sems.at[n])]
        if n != 2:
            target = outs[(0, 1, None, 4)[n]]
            return [pltpu.make_async_copy(result.at[n], target, store_sems.at[n])]
        cut = chunk // 2
        top, bottom = pl.ds(0, cut), pl.ds(cut, cut)
        return [
            pltpu.make_async_copy(result.at[n, top], outs[2], store_sems.at[n]),
            pltpu.make_async_copy(result.at[n, bottom], outs[3], store_sems.at[RING]),
        ]

    each = [(k, h) for k in range(RING) for h in range(2)]
    order = (2, 1, 3, 0)
    for copy in right_loads():
        copy.start()
    for n in order:
        for k, h in each:
            left_load(n, k, h).start()
    for copy in right_loads():
        copy.wait()
    for n in order:
        for k, h in each:
            left_load(n, k, h).wait()
        for columns in (slice(0, wide), slice(wide, width)):
            total = dot(left[n], right[:, columns], ((0,), (0,)))
            if not first:
                total = total + rest[0][n, :, columns].astype(F32)
            result[n, :, columns] = total.astype(BF)
        for copy in stores(n):
            copy.start()
    for n in order:
        for copy in stores(n):
            copy.wait()


def weight_grad(where, lefts, rights, so_far=None, after=()):
    halves, rows, part = lefts[0].shape
    width = rights[0].shape[1]
    chunk, pieces = part // RING, len(rights)
    first = so_far is None
    whole = (RING, chunk, width)
    heights = [chunk, chunk, chunk // 2, chunk // 2, chunk]
    outs = [shape(whole)] if first else [shape((height, width)) for height in heights]
    return call(
        functools.partial(weight_grad_body, first, pieces),
        (1,),
        [where],
        [*lefts, *rights] + ([] if first else [so_far]),
        [ANYWHERE] * (RING + pieces)
        + ([] if first else [pl.BlockSpec(whole, lambda i, where_ref: (0, 0, 0))]),
        outs,
        [ANYWHERE] * len(outs),
        scratch=[
            pltpu.VMEM((RING, RING * halves * rows, chunk), BF),
            pltpu.VMEM((RING * halves * rows, width), BF),
            pltpu.VMEM(whole, BF),
            pltpu.SemaphoreType.DMA((RING, RING, 2)),
            pltpu.SemaphoreType.DMA((pieces,)),
            pltpu.SemaphoreType.DMA((RING + 1,)),
        ],
        after=after,
        cost_estimate=cost(0, 0),
    )


def relay_body(up_ref, got_up_ref, down_ref, got_down_ref, up_out, down_out):
    cut = got_up_ref.shape[0]
    up_out[:cut] = (up_ref[:cut].astype(F32) + got_up_ref[...].astype(F32)).astype(BF)
    up_out[cut:] = up_ref[cut:]
    down_out[:cut] = down_ref[:cut]
    down_out[cut:] = (down_ref[cut:].astype(F32) + got_down_ref[...].astype(F32)).astype(BF)


def relay(up, got_up, down, got_down):
    whole = pl.BlockSpec(up.shape, lambda i: (0, 0))
    half = pl.BlockSpec(got_up.shape, lambda i: (0, 0))
    return call(
        relay_body,
        (1,),
        [],
        [up, got_up, down, got_down],
        [whole, half, whole, half],
        [shape(up.shape)] * 2,
        [whole, whole],
        cost_estimate=cost(0, 0),
    )


def later(array, after):
    return call(
        lambda *refs: None,
        (1,),
        [],
        [array],
        [ANYWHERE],
        shape(array.shape, array.dtype),
        ANYWHERE,
        after=after,
        input_output_aliases={0: 0},
    )


def hop(first, distance):
    pairs = []
    for z in range(RING):
        for y in range(RING):
            for core in range(2):
                along_y = (core == 0) == first
                to = (z, (y + distance) % RING) if along_y else ((z + distance) % RING, y)
                pairs.append(((z * RING + y) * 2 + core, (to[0] * RING + to[1]) * 2 + core))
    return pairs


def rotate(array, first, distance):
    return lax.ppermute(array, ("z", "y", "c"), hop(first, distance))


def local(
    vit_partial,
    vit_residual,
    ln_gain,
    key_weight,
    value_weight,
    queries,
    context_grad,
    text_len,
    image_pick,
):
    share, model_width = vit_residual.shape
    width = key_weight.shape[1]
    core, side, cross = lax.axis_index("c"), lax.axis_index("xl"), lax.axis_index("xh")
    y, z = lax.axis_index("y"), lax.axis_index("z")
    where = jnp.stack([core, side, jnp.where(core == 0, y, z), jnp.where(core == 0, z, y), cross])
    pick = image_pick[0]
    gain = ln_gain[None, :]

    mine, other, after = [], [], []
    for image in range(2):
        sent = part_of(image, where, vit_partial, vit_residual, after)
        after = [sent]
        theirs = lax.ppermute(sent, "c", SWAP)
        mine.append(chip_sum(image, where, vit_partial, theirs, vit_residual))
        other.append(lax.ppermute(mine[image], "xl", SWAP))

    def spread(array, firsts):
        return [array] + [rotate(firsts[k], True, k) for k in range(1, RING)]

    def core_sum(near_rows, away_rows):
        theirs = lax.ppermute(away_rows, "c", SWAP)
        return (near_rows.astype(F32) + theirs.astype(F32)).astype(BF)

    def step(image, own, far, texts, after):
        given = (key_weight, value_weight, queries, context_grad)
        return image_step(image, pick, text_len, own, far, *given, texts, after)

    own = norm(mine[0], other[0], gain, [mine[1]])
    far = lax.ppermute(own, "c", SWAP)
    pieces = strips(where, own, far, [])
    lefts = spread(pieces[0], pieces)
    *texts, near_rows, away_rows, grads = step(0, own, far, [], [pieces[0]])
    grads = later(grads, [lefts[1], lefts[3]])
    rights = spread(grads, [grads] * RING)

    own = norm(mine[1], other[1], gain, [near_rows, lefts[2], *rights[1:]])
    far = lax.ppermute(own, "c", SWAP)
    pieces = strips(where, own, far, [])
    last_lefts = spread(pieces[0], pieces)
    near_0, away_0 = near_rows, away_rows
    *texts, near_rows, away_rows, grads = step(1, own, far, texts, [pieces[0]])
    share_0 = core_sum(near_0, later(away_0, [pieces[0]]))
    grads = later(grads, [last_lefts[1], last_lefts[3]])
    last_rights = spread(grads, [grads] * RING)
    (so_far,) = weight_grad(where, lefts, rights, after=[grads, share_0, last_lefts[2]])
    share_1 = core_sum(near_rows, later(away_rows, [grads]))

    from_second = lax.ppermute(share_0, "xl", [(1, 0)])
    from_first = lax.ppermute(share_1, "xl", [(0, 1)])
    blocks = weight_grad(where, last_lefts, last_rights, so_far, [share_0, share_1])
    kept, up, across_up, across_down, down = blocks
    got_up = rotate(across_up, False, 1)
    got_down = rotate(across_down, False, RING - 1)
    up, down = relay(up, got_up, down, got_down)
    got = [rotate(up, False, 1), rotate(down, False, RING - 1)]
    stream_grad = norm_back(
        where,
        gain,
        [mine[0], other[0], share_0, from_second],
        [mine[1], other[1], share_1, from_first],
    )
    kept, sent = ring_sum(where, [kept, *got], [from_first, from_second])
    got = lax.ppermute(sent, "xh", SWAP)
    key_weight_grad, value_weight_grad = last_sum(kept, got, [stream_grad])
    return texts[0], texts[1], key_weight_grad, value_weight_grad, stream_grad


def solution(mesh):
    fine = Mesh(mesh.devices.reshape(4, 2, 4, 2, 2), ("z", "xh", "y", "xl", "c"))
    dp, mp = ("z", "xh", "y"), ("xl", "c")
    placed = (
        P(mp, dp, None),
        P(dp + mp, None),
        P(),
        P(None, mp),
        P(None, mp),
        P(dp, None, mp),
        P(dp, None, mp),
        P(dp),
        P(dp, None),
    )
    return jax.shard_map(
        local,
        mesh=fine,
        in_specs=placed,
        out_specs=(P(dp, None, mp), P(dp, None, mp), P(dp, mp), P(dp, mp), P(dp + mp, None)),
        check_vma=False,
    )
```
